256 devices in a mesh: pb: 16 (over z, core), pa: 16 (over y, x).
Axes of the slice: x: 4, y: 4, z: 8, core: 2. Of those that a mesh axis runs over, the one named last changes fastest.
Arguments:
- query_hidden: bfloat16 [4096, 32, 4096], P(('pb', 'pa')), may hold values from -6 to 6
- passage_hidden: bfloat16 [768, 256, 4096], P(('pb', 'pa')), may hold values from -6 to 6
- projection: bfloat16 [4096, 128], replicated, may hold values from -0.09375 to 0.09375
- candidates: int32 [4096, 9], P(('pb', 'pa')), may hold values from 0 to 47, all different within a row; in each aligned block of 16 rows (0 to 15, 16 to 31, ...) at most 5 rows name the same one
Outputs:
- query_loss: float32 [4096], P(('pb', 'pa'))
- query_grad: float32 [4096, 32, 128], P(('pb', 'pa'))
- passage_grad: float32 [768, 256, 128], P(('pb', 'pa'))
- weight_grad: float32 [4096, 128], replicated
The draws below stay inside these ranges and needn't reach their ends.
Inputs may be any that keep to these rules, and one draw needn't show every extreme that they name: `candidates`: the 9 numbers of a query are different. Among the 16 queries of one device (aligned blocks of rows) no passage is named more than 5 times, and in every draw some passage is named exactly 5 times by some device's queries.
All inputs are finite; a program needn't handle non-finite values.
Results may differ from the reference program's by a relative error of at most 0.015.
Values may be sent and summed in bfloat16 or wider, within the bound.
A program may use at most 128 MiB of HBM per device.

```python
import math
import jax
import jax.numpy as jnp
import numpy as np
from jax import lax

D = 4096
VECTOR_DIMENSION = 128
QLEN = 32
PLEN = 256
CANDS = 9
Q_DEV = 16
P_GRP = 48
MOST = 5
QUERIES = 4096
PASSAGES = 768
N_PA = 16


def level_of(key, shape, split, smallest, top_value):
    factor_of = 1.0
    for position, parts in split:
        draws = jax.random.uniform(jax.random.fold_in(jax.random.fold_in(key, 6), position), (parts,), jnp.float32, smallest / len(split), top_value / len(split))
        factor_of = factor_of * jnp.repeat(jnp.exp(draws), shape[position] // parts).reshape((-1,) + (1,) * (len(shape) - 1 - position))
    return factor_of


def routed_block(key, own, number, rows, count, top, limit, slope):
    sequence = jax.random.permutation(key, count)
    crowded, usual = load_shares(count, rows * top, limit, slope, True), load_shares(count, rows * top, limit, slope, False)
    places = jnp.arange(count)

    def named(sizes, rotation):
        used = int((sizes > 0).sum())
        fixed = max(1, used // 4)
        shifted = fixed + (places - fixed + rotation * (used - fixed)) % max(1, count - fixed)
        return jnp.zeros((count,), jnp.int32).at[sequence[jnp.where(places < fixed, places, shifted)]].set(jnp.asarray(sizes, jnp.int32))

    sizes = jnp.where(number % 4 == 0, named(crowded, number // 4), named(usual, number - number // 4 - 1))
    mixed = jax.random.permutation(jax.random.fold_in(own, 3), count)
    giver, receiver = mixed[0:count // 2 * 2:2], mixed[1:count // 2 * 2:2]
    slack = jnp.minimum(sizes[giver] - 1, limit - sizes[receiver]) // 2
    slack = jnp.where((giver == sequence[0]) | (receiver == sequence[0]) | (sizes[receiver] == 0), 0, jnp.maximum(slack, 0))
    shifted = jax.random.randint(jax.random.fold_in(own, 4), (count // 2,), 0, 1 << 20) % (slack + 1)
    sizes = sizes.at[giver].add(-shifted).at[receiver].add(shifted)
    items = jnp.searchsorted(jnp.cumsum(sizes), jnp.arange(rows * top), side="right").astype(jnp.int32)
    listing = items.reshape(top, rows).T
    listing = listing[jax.random.permutation(jax.random.fold_in(own, 1), rows)]
    rotation = jax.random.randint(jax.random.fold_in(own, 2), (rows, 1), 0, top)
    return jnp.take_along_axis(listing, (jnp.arange(top)[None, :] + rotation) % top, axis=1)


def load_shares(count, total, most, skew, full):
    portions = [(1 << 20) // math.isqrt(standing ** skew) + 1 for standing in range(1, count + 1)]
    largest = most if full else min(most, max(-(-total // count), total * portions[0] // sum(portions)))
    least = 1 if total - largest >= count - 1 else 0
    counts, surplus = [largest] + [least] * (count - 1), total - largest - least * (count - 1)
    while surplus > 0:
        free = [i for i in range(1, count) if counts[i] < largest] or [i for i in range(1, count) if counts[i] < most]
        mass, remaining = sum([portions[i] for i in free]), surplus
        for i in free:
            addition = min(most - counts[i], max(1, remaining * portions[i] // mass), surplus)
            counts[i] = counts[i] + addition
            surplus = surplus - addition
    return np.array(counts)


def centred(own_key, extent, spread, most, cuts=(), kind=jnp.bfloat16):
    values = jax.random.normal(own_key, extent, jnp.float32) * spread
    if len(cuts) > 0:
        values = level_of(own_key, extent, cuts, -0.22, 0.18) * values
    return jnp.clip(values, min=-most, max=most).astype(kind)


def setup_inputs(seed: int = 0) -> dict:
    seeds = jax.random.split(jax.random.key(seed), 5)
    query_hidden = centred(seeds[0], (QUERIES, QLEN, D), 1.0, 6.0, ((0, 256),))
    passage_hidden = centred(seeds[1], (PASSAGES, PLEN, D), 1.0, 6.0, ((0, 256),))
    projection = centred(seeds[2], (D, VECTOR_DIMENSION), D ** -0.5, 0.09375)
    candidates_keys = jax.random.split(jax.random.fold_in(seeds[3], 1), QUERIES // Q_DEV)
    candidates_turns = jax.random.permutation(jax.random.fold_in(seeds[3], 3), QUERIES // Q_DEV)
    candidates = jax.vmap(lambda own, number: routed_block(jax.random.fold_in(seeds[3], 2), own, number, Q_DEV, P_GRP, CANDS, MOST, 2))(candidates_keys, candidates_turns).reshape((QUERIES, CANDS))
    return dict(query_hidden=query_hidden, passage_hidden=passage_hidden, projection=projection, candidates=candidates)


sharpness_divisor = 0.1
epsilon = 1e-06

def project_rows(hidden, projection):
    flattened = hidden.reshape(-1, hidden.shape[-1])
    embedded = jnp.dot(flattened, projection, preferred_element_type=jnp.float32)
    inv_norm = lax.rsqrt(lax.optimization_barrier(jnp.mean(embedded * embedded, axis=-1, keepdims=True)) + epsilon)
    return (embedded, inv_norm, (embedded * inv_norm).astype(jnp.bfloat16))

def norm_backward(embedded, inv_norm, unit_grad):
    inner_mean = lax.optimization_barrier(jnp.mean(embedded * unit_grad, axis=-1, keepdims=True))
    return inv_norm * unit_grad - inv_norm * inv_norm * inv_norm * embedded * inner_mean

def contrast_loss(pairwise_similarity, positive):
    exponent = jnp.exp(pairwise_similarity)
    element_total = lax.optimization_barrier(jnp.sum(exponent, axis=-1, keepdims=True))
    query_loss = jnp.log(element_total[:, 0]) - pairwise_similarity[:, 0]
    return (query_loss, exponent / element_total - positive)

def reference(query_hidden, passage_hidden, projection, candidates):
    q_embed, q_norm, q_unit = project_rows(query_hidden, projection)
    p_embed, p_norm, p_unit = project_rows(passage_hidden, projection)
    query_units = q_unit.reshape(QUERIES, QLEN, VECTOR_DIMENSION)
    passage_units = p_unit.reshape(PASSAGES, PLEN, VECTOR_DIMENSION)
    group_index = jnp.arange(QUERIES, dtype=jnp.int32) // (Q_DEV * N_PA)
    named = (candidates + (group_index * P_GRP)[:, None]).astype(jnp.int32)
    blocks = QUERIES // Q_DEV
    positive = (jnp.arange(CANDS) == 0).astype(jnp.float32)

    def block_step(accumulated, inputs):
        unit_rows, block_ids = inputs
        chosen_passage = passage_units[block_ids.reshape(-1)].reshape(Q_DEV, CANDS, PLEN, VECTOR_DIMENSION).astype(jnp.float32)
        question_group = unit_rows.astype(jnp.float32)
        affinity_values = jnp.einsum('nat,nrlt->nral', question_group, chosen_passage) / (VECTOR_DIMENSION * sharpness_divisor)
        exponent = jnp.exp(affinity_values)
        element_total = lax.optimization_barrier(jnp.sum(exponent, axis=-1, keepdims=True))
        weights = exponent / element_total
        pairwise_similarity = sharpness_divisor * lax.optimization_barrier(jnp.sum(jnp.log(element_total[..., 0]), axis=-1))
        query_loss, grad_score = contrast_loss(pairwise_similarity, positive)
        weighted = (grad_score[..., None, None] * weights / VECTOR_DIMENSION).astype(jnp.bfloat16).astype(jnp.float32)
        grad_query = jnp.einsum('qcij,qcje->qie', weighted, chosen_passage)
        partial_terms = jnp.einsum('qcij,qie->qcje', weighted, question_group)
        accumulated = accumulated.at[block_ids.reshape(-1)].add(partial_terms.reshape(-1, PLEN, VECTOR_DIMENSION))
        return (accumulated, (query_loss, grad_query))
    start = jnp.zeros((PASSAGES, PLEN, VECTOR_DIMENSION), jnp.float32)
    inputs = (query_units.reshape(blocks, Q_DEV, QLEN, VECTOR_DIMENSION), named.reshape(blocks, Q_DEV, CANDS))
    grad_p, (losses, grad_q) = lax.scan(block_step, start, inputs)
    query_grad = norm_backward(q_embed, q_norm, grad_q.reshape(-1, VECTOR_DIMENSION))
    passage_grad = norm_backward(p_embed, p_norm, grad_p.reshape(-1, VECTOR_DIMENSION))
    q_flat = query_hidden.reshape(-1, D)
    p_flat = passage_hidden.reshape(-1, D)
    contract = (((0,), (0,)), ((), ()))
    weight_grad = lax.dot_general(q_flat, query_grad.astype(jnp.bfloat16), contract, preferred_element_type=jnp.float32)
    weight_grad = weight_grad + lax.dot_general(p_flat, passage_grad.astype(jnp.bfloat16), contract, preferred_element_type=jnp.float32)
    return (losses.reshape(QUERIES), query_grad.reshape(QUERIES, QLEN, VECTOR_DIMENSION), passage_grad.reshape(PASSAGES, PLEN, VECTOR_DIMENSION), weight_grad)
```

```python
import functools
import jax
import jax.numpy as jnp
from jax import lax
from jax.experimental import pallas as pl
from jax.experimental.pallas import tpu as pltpu

from jax.sharding import PartitionSpec as P

MESH = pl.DeviceIdType.MESH
F32, BF16 = jnp.float32, jnp.bfloat16


def remote(src, dst, send, recv, device):
    return pltpu.make_async_remote_copy(
        src_ref=src, dst_ref=dst, send_sem=send, recv_sem=recv, device_id=device, device_id_type=MESH
    )


def sum_kernel(n_pa, n_z, g_ref, o_ref, out, half, got0, part, got1, mine, got2,
               s0, r0, s1, r1, s2, r2, s3, r3, s4, r4, s5, r5):
    rows = g_ref.shape[0]
    half_rows = rows // 2
    chunk = half_rows // n_pa
    piece = chunk // n_z
    pa, pb = lax.axis_index("pa"), lax.axis_index("pb")
    z, core = pb // 2, pb % 2
    partner = {"pb": z * 2 + (1 - core)}
    base = core * half_rows

    def xy(k):
        return lax.rem(pa + k, n_pa)

    def zz(k):
        return lax.rem(z + k, n_z)

    barrier = pltpu.get_barrier_semaphore()
    pl.semaphore_signal(barrier, inc=1, device_id=partner, device_id_type=MESH)

    @pl.loop(1, n_pa)
    def _(k):
        pl.semaphore_signal(barrier, inc=1, device_id={"pa": xy(k)}, device_id_type=MESH)

    @pl.loop(1, n_z)
    def _(k):
        pl.semaphore_signal(barrier, inc=1, device_id={"pb": zz(k) * 2 + core}, device_id_type=MESH)

    half[...] = g_ref[pl.ds((1 - core) * half_rows, half_rows), :].astype(BF16)
    pl.semaphore_wait(barrier, n_pa + n_z - 1)

    def swap(k):
        at = pl.ds(xy(k) * chunk, chunk)
        return remote(half.at[at], got0.at[at], s0.at[k], r0.at[k], partner)

    def to_xy(k):
        return remote(part.at[xy(k)], got1.at[pa], s1.at[k], r1.at[n_pa - k], {"pa": xy(k)})

    @pl.loop(0, n_pa)
    def _(k):
        swap(lax.rem(k + 1, n_pa)).start()

    @pl.loop(1, n_pa)
    def _(k):
        peer = xy(k)
        swap(k).wait_recv()
        mix = g_ref[pl.ds(base + peer * chunk, chunk), :] + got0[pl.ds(peer * chunk, chunk), :].astype(F32)
        part[peer] = mix.astype(BF16)
        to_xy(k).start()

    swap(0).wait_recv()
    mine[...] = g_ref[pl.ds(base + pa * chunk, chunk), :] + got0[pl.ds(pa * chunk, chunk), :].astype(F32)

    @pl.loop(1, n_pa)
    def _(k):
        remote(part.at[xy(k)], got1.at[xy(k)], s1.at[k], r1.at[k], {"pa": xy(k)}).wait_recv()
        mine[...] += got1[xy(k)].astype(F32)

    part[pa] = mine[...].astype(BF16)

    def to_z(k):
        return remote(part.at[pa, pl.ds(zz(k) * piece, piece)], got2.at[z], s2.at[k], r2.at[n_z - k],
                      {"pb": zz(k) * 2 + core})

    @pl.loop(1, n_z)
    def _(k):
        to_z(k).start()

    total = mine[pl.ds(z * piece, piece), :]
    for k in range(1, n_z):
        remote(part.at[pa, pl.ds(0, piece)], got2.at[zz(k)], s2.at[k], r2.at[k], {"pb": zz(k) * 2 + core}).wait_recv()
        total = total + got2[zz(k)].astype(F32)
    at_z = pl.ds(base + pa * chunk + z * piece, piece)
    out[at_z, :] = total.astype(BF16)

    def back_z(k, who):
        at = pl.ds(base + pa * chunk + who * piece, piece)
        return remote(out.at[at], out.at[at], s3.at[k], r3.at[n_z - k], {"pb": zz(k) * 2 + core})

    @pl.loop(1, n_z)
    def _(k):
        back_z(k, z).start()

    @pl.loop(1, n_z)
    def _(k):
        at = pl.ds(base + pa * chunk + zz(k) * piece, piece)
        remote(out.at[at], out.at[at], s3.at[k], r3.at[k], {"pb": zz(k) * 2 + core}).wait_recv()

    at_pa = pl.ds(base + pa * chunk, chunk)

    @pl.loop(1, n_pa)
    def _(k):
        remote(out.at[at_pa], out.at[at_pa], s4.at[k], r4.at[n_pa - k], {"pa": xy(k)}).start()

    def across(k, first):
        at = pl.ds(first + xy(k) * chunk, chunk)
        return remote(out.at[at], out.at[at], s5.at[k], r5.at[k], partner)

    across(0, base).start()

    @pl.loop(1, n_pa)
    def _(k):
        at = pl.ds(base + xy(k) * chunk, chunk)
        remote(out.at[at], out.at[at], s4.at[k], r4.at[k], {"pa": xy(k)}).wait_recv()
        across(k, base).start()

    @pl.loop(0, n_pa)
    def _(k):
        across(k, half_rows - base).wait_recv()

    @pl.loop(0, n_pa)
    def _(k):
        swap(k).wait_send()
        across(k, base).wait_send()

    @pl.loop(1, n_pa)
    def _(k):
        to_xy(k).wait_send()
        remote(out.at[at_pa], out.at[at_pa], s4.at[k], r4.at[k], {"pa": xy(k)}).wait_send()

    @pl.loop(1, n_z)
    def _(k):
        to_z(k).wait_send()
        back_z(k, z).wait_send()

    o_ref[...] = out[...]


def sum_all(g, n_pa, n_z):
    rows, width = g.shape
    chunk = rows // 2 // n_pa
    piece = chunk // n_z
    dma = pltpu.SemaphoreType.DMA
    return pl.pallas_call(
        functools.partial(sum_kernel, n_pa, n_z),
        out_shape=jax.ShapeDtypeStruct((rows, width), BF16),
        in_specs=[pl.BlockSpec(memory_space=pltpu.VMEM)],
        out_specs=pl.BlockSpec(memory_space=pltpu.VMEM),
        scratch_shapes=[
            pltpu.VMEM((rows, width), BF16),
            pltpu.VMEM((rows // 2, width), BF16),
            pltpu.VMEM((rows // 2, width), BF16),
            pltpu.VMEM((n_pa, chunk, width), BF16),
            pltpu.VMEM((n_pa, chunk, width), BF16),
            pltpu.VMEM((chunk, width), F32),
            pltpu.VMEM((n_z, piece, width), BF16),
            dma((n_pa,)), dma((n_pa,)), dma((n_pa,)), dma((n_pa,)), dma((n_z,)), dma((n_z,)),
            dma((n_z,)), dma((n_z,)), dma((n_pa,)), dma((n_pa,)), dma((n_pa,)), dma((n_pa,)),
        ],
        compiler_params=pltpu.CompilerParams(collective_id=0, has_side_effects=True, vmem_limit_bytes=32 * 2**20),
        name="sum_devices",
    )(g)

sharpness_divisor = 0.1
epsilon = 1e-06


def project_rows(hidden, projection):
    flattened = hidden.reshape(-1, hidden.shape[-1])
    embedded = jnp.dot(flattened, projection, preferred_element_type=jnp.float32)
    inv_norm = lax.rsqrt(jnp.mean(embedded * embedded, axis=-1, keepdims=True) + epsilon)
    return (embedded, inv_norm, (embedded * inv_norm).astype(jnp.bfloat16))


def norm_backward(embedded, inv_norm, unit_grad):
    inner_mean = jnp.mean(embedded * unit_grad, axis=-1, keepdims=True)
    return inv_norm * unit_grad - inv_norm * inv_norm * inv_norm * embedded * inner_mean


def contrast_loss(pairwise_similarity, positive):
    exponent = jnp.exp(pairwise_similarity)
    element_total = jnp.sum(exponent, axis=-1, keepdims=True)
    query_loss = jnp.log(element_total[:, 0]) - pairwise_similarity[:, 0]
    return (query_loss, exponent / element_total - positive)


def shards(query_hidden, passage_hidden, projection, candidates):
    query_count, query_len, feature_width = query_hidden.shape
    passage_count, passage_len, _ = passage_hidden.shape
    vector_dimension = projection.shape[1]
    cand_count = candidates.shape[1]
    shard_count = lax.axis_size("pa")
    group_total = passage_count * shard_count
    q_embed, q_norm, q_unit = project_rows(query_hidden, projection)
    p_embed, p_norm, p_unit = project_rows(passage_hidden, projection)
    passage_units = p_unit.reshape(passage_count, passage_len, vector_dimension)
    positive = (jnp.arange(cand_count) == 0).astype(jnp.float32)
    flat_ids = candidates.reshape(-1)
    divisor_total = vector_dimension * sharpness_divisor
    slot_most = max(
        2,
        min(query_count, (3 * query_count * cand_count + 2 * group_total - 1) // (2 * group_total)),
    )
    slot_count = group_total * slot_most
    marks = (flat_ids[:, None] == jnp.arange(group_total, dtype=jnp.int32)[None, :]).astype(
        jnp.int32
    )
    earlier = jnp.sum((jnp.cumsum(marks, axis=0) - marks) * marks, axis=1)
    slot_index = flat_ids * slot_most + earlier
    dispatch = (jnp.arange(slot_count, dtype=jnp.int32)[:, None] == slot_index[None, :]).astype(
        jnp.float32
    )
    by_query = jnp.sum(dispatch.reshape(slot_count, query_count, cand_count), axis=2)
    outgoing = jnp.dot(
        by_query.astype(jnp.bfloat16),
        q_unit.reshape(query_count, query_len * vector_dimension),
        preferred_element_type=jnp.float32,
    ).astype(jnp.bfloat16)
    outgoing = outgoing.reshape(
        shard_count, passage_count * slot_most, query_len * vector_dimension
    )
    arrived = lax.all_to_all(outgoing, "pa", split_axis=0, concat_axis=0, tiled=True)
    arrived = arrived.reshape(shard_count, passage_count, slot_most, query_len, vector_dimension)
    affinity_values = (
        jnp.einsum("spmie,pje->spmij", arrived, passage_units, preferred_element_type=jnp.float32)
        / divisor_total
    )
    exponent = jnp.exp(affinity_values)
    element_total = jnp.sum(exponent, axis=-1, keepdims=True)
    weights = exponent / element_total
    passage_position_affinity = sharpness_divisor * jnp.sum(jnp.log(element_total[..., 0]), axis=-1)
    returned = lax.all_to_all(
        passage_position_affinity.reshape(shard_count, passage_count * slot_most),
        "pa",
        split_axis=0,
        concat_axis=0,
        tiled=True,
    )
    pairwise_similarity = jnp.dot(
        returned.reshape(slot_count), dispatch, precision=lax.Precision.HIGHEST
    ).reshape(query_count, cand_count)
    query_loss, grad_score = contrast_loss(pairwise_similarity, positive)
    slot_grad = jnp.dot(dispatch, grad_score.reshape(-1), precision=lax.Precision.HIGHEST)
    slot_back = lax.all_to_all(
        slot_grad.reshape(shard_count, passage_count * slot_most),
        "pa",
        split_axis=0,
        concat_axis=0,
        tiled=True,
    )
    slot_back = slot_back.reshape(shard_count, passage_count, slot_most)
    weighted = (slot_back[..., None, None] * weights / vector_dimension).astype(jnp.bfloat16)
    slot_query = jnp.einsum(
        "spmij,pje->spmie", weighted, passage_units, preferred_element_type=jnp.float32
    )
    grad_p = jnp.einsum("spmij,spmie->pje", weighted, arrived, preferred_element_type=jnp.float32)
    returned_grads = lax.all_to_all(
        slot_query.reshape(
            shard_count, passage_count * slot_most, query_len * vector_dimension
        ).astype(jnp.bfloat16),
        "pa",
        split_axis=0,
        concat_axis=0,
        tiled=True,
    ).astype(jnp.float32)
    grad_q = lax.dot_general(
        by_query,
        returned_grads.reshape(slot_count, query_len * vector_dimension),
        (((0,), (0,)), ((), ())),
        precision=lax.Precision.HIGHEST,
    )
    query_grad = norm_backward(q_embed, q_norm, grad_q.reshape(-1, vector_dimension))
    passage_grad = norm_backward(p_embed, p_norm, grad_p.reshape(-1, vector_dimension))
    contract = (((0,), (0,)), ((), ()))
    local_sum = lax.dot_general(
        query_hidden.reshape(-1, feature_width),
        query_grad.astype(jnp.bfloat16),
        contract,
        preferred_element_type=jnp.float32,
    )
    local_sum = local_sum + lax.dot_general(
        passage_hidden.reshape(-1, feature_width),
        passage_grad.astype(jnp.bfloat16),
        contract,
        preferred_element_type=jnp.float32,
    )
    weight_grad = sum_all(local_sum, lax.axis_size("pa"), lax.axis_size("pb") // 2).astype(F32)
    return (
        query_loss,
        query_grad.reshape(query_count, query_len, vector_dimension),
        passage_grad.reshape(passage_count, passage_len, vector_dimension),
        weight_grad,
    )


def solution(mesh):
    placed = (P(("pb", "pa"), None, None), P(("pb", "pa"), None, None), P(), P(("pb", "pa"), None))
    return jax.shard_map(
        shards,
        mesh=mesh,
        in_specs=placed,
        out_specs=(P(("pb", "pa")), P(("pb", "pa"), None, None), P(("pb", "pa"), None, None), P()),
        check_vma=False,
    )
```

```python
import functools
import jax
import jax.numpy as jnp
from jax import lax
from jax.experimental import pallas as pl
from jax.experimental.pallas import tpu as pltpu
from jax.sharding import PartitionSpec as P

MESH = pl.DeviceIdType.MESH
F32, BF16 = jnp.float32, jnp.bfloat16
SIDE = 4
sharpness_divisor = 0.1
epsilon = 1e-06
LOG2E = 1.4426950408889634


def remote(src, dst, send, recv, device):
    return pltpu.make_async_remote_copy(
        src_ref=src, dst_ref=dst, send_sem=send, recv_sem=recv, device_id=device, device_id_type=MESH
    )


def dot(a, b, ca=1, cb=0):
    return lax.dot_general(a, b, (((ca,), (cb,)), ((), ())), preferred_element_type=F32)


def inverse_norm(embedded):
    return lax.rsqrt(jnp.mean(embedded * embedded, axis=-1, keepdims=True) + epsilon)


def norm_backward(embedded, unit_grad):
    inv_norm = inverse_norm(embedded)
    inner_mean = jnp.mean(embedded * unit_grad, axis=-1, keepdims=True)
    return inv_norm * unit_grad - inv_norm * inv_norm * inv_norm * embedded * inner_mean


def pick(k, values):
    result = jnp.int32(values[0])
    for i, v in enumerate(values[1:]):
        result = jnp.where(k == i + 1, jnp.int32(v), result)
    return result


ORDER = [(0, 0), (1, 0), (3, 0), (0, 1), (0, 3), (1, 1), (1, 3), (3, 1), (3, 3),
         (2, 0), (0, 2), (2, 1), (2, 3), (1, 2), (3, 2), (2, 2)]


def kernel(n_z, qlen, cand_count,
           qh_ref, ph_ref, proj_ref, cand_ref,
           loss_ref, qg_ref, pg_ref, wg_ref,
           qh, ph, qe, pe, pt, pone, gq, ex, gn, qn, acc, cbuf, mask, mark, score, gsrep,
           sbuf1, sbuf2, rbuf1, rbuf2, sum1, gp, qgb, pgb,
           wg, out, half, got0, part, got1, mine, got2,
           sem_h, c_s, c_r, sc_s, sc_r, a_s, a_r, b_s, b_r,
           s0, r0, s1, r1, s2, r2, s3, r3, s4, r4, s5, r5):
    n_pa = SIDE * SIDE
    rows_q = qh.shape[0]
    hrow = rows_q // 2
    qrow = hrow // 2
    queries = rows_q // qlen
    n_p, plen = pone.shape[0], pone.shape[1]
    width = qh.shape[1]
    vec = proj_ref.shape[1]
    me, pb = lax.axis_index("pa"), lax.axis_index("pb")
    y, x = me // SIDE, me % SIDE
    z, core = pb // 2, pb % 2
    partner = {"pb": z * 2 + (1 - core)}
    scale = 1.0 / (vec * sharpness_divisor)

    def xy(k):
        return lax.rem(me + k, n_pa)

    def zz(k):
        return lax.rem(z + k, n_z)

    def load_q(k):
        at = pl.ds(k * hrow, hrow)
        return pltpu.make_async_copy(qh_ref.at[at], qh.at[at], sem_h.at[k])

    def load_p(k):
        at = pl.ds(k * plen, plen)
        return pltpu.make_async_copy(ph_ref.at[at], ph.at[at], sem_h.at[2 + k])

    for k in range(2):
        load_q(k).start()
    for k in range(n_p):
        load_p(k).start()

    barrier = pltpu.get_barrier_semaphore()
    pl.semaphore_signal(barrier, inc=1, device_id=partner, device_id_type=MESH)

    @pl.loop(1, n_pa)
    def _(k):
        pl.semaphore_signal(barrier, inc=1, device_id={"pa": xy(k)}, device_id_type=MESH)

    @pl.loop(1, n_z)
    def _(k):
        pl.semaphore_signal(barrier, inc=1, device_id={"pb": zz(k) * 2 + core}, device_id_type=MESH)

    lane = lax.broadcasted_iota(jnp.int32, (128, 128), 1)
    line = lax.broadcasted_iota(jnp.int32, (128, 128), 0)
    place = (lane == line + (me % 8) * queries).astype(F32) * (line < queries).astype(F32)
    cbuf[me] = dot(cand_ref[...], place)
    score[...] = jnp.zeros_like(score)
    acc[...] = jnp.zeros_like(acc)

    def slot(h, d1, d2):
        dx, dy = d1 * (1 - h) + d2 * h, d2 * (1 - h) + d1 * h
        return lax.rem(y + dy, SIDE) * SIDE + lax.rem(x + dx, SIDE)

    def offset(h, g, o):
        first = jnp.int32(g == 0) if isinstance(g, int) else (g == 0).astype(jnp.int32)
        d1 = first * o + (1 - first) * (g - 1)
        return d1, (1 - first) * o

    def neighbour(h, g, o):
        first = jnp.int32(g == 0) if isinstance(g, int) else (g == 0).astype(jnp.int32)
        return {"pa": slot(h, first * o, (1 - first) * o)}

    def whole(h, g, o, k, to):
        block = gq.at[slot(h, *offset(h, g, o)), pl.ds(h * hrow, hrow)]
        i = (h * 5 + g) * 4 + k
        return remote(block, block, a_s.at[i], a_r.at[i], neighbour(h, g, to))

    def quarter(h, g, o, k, to):
        block = gq.at[slot(h, *offset(h, g, o)), pl.ds(h * hrow + (k - 2) * qrow, qrow)]
        i = (h * 5 + g) * 4 + k
        return remote(block, block, a_s.at[i], a_r.at[i], neighbour(h, g, to))

    def send_whole(h, g):
        whole(h, g, 0, 0, 1).start()
        whole(h, g, 0, 1, 3).start()

    def pass_on(h, g):
        whole(h, g, 3, 0, 1).wait_recv()
        quarter(h, g, 3, 2, 1).start()
        whole(h, g, 1, 1, 3).wait_recv()
        quarter(h, g, 1, 3, 3).start()

    def finish(h, g):
        quarter(h, g, 2, 2, 1).wait_recv()
        quarter(h, g, 2, 3, 3).wait_recv()

    def sent(h, g):
        whole(h, g, 0, 0, 1).wait_send()
        whole(h, g, 0, 1, 3).wait_send()
        quarter(h, g, 3, 2, 1).wait_send()
        quarter(h, g, 1, 3, 3).wait_send()

    def to_all(buf, send, recv, k):
        return remote(buf.at[me], buf.at[me], send.at[k], recv.at[n_pa - k], {"pa": xy(k)})

    def from_all(buf, send, recv, k):
        return remote(buf.at[xy(k)], buf.at[xy(k)], send.at[k], recv.at[k], {"pa": xy(k)})

    for h in range(2):
        at = pl.ds(h * hrow, hrow)
        load_q(h).wait()
        e = dot(qh[at, :], proj_ref[...])
        qe[at, :] = e
        gq[me, at, :] = (e * inverse_norm(e)).astype(BF16)
        if h == 0:
            pl.semaphore_wait(barrier, n_pa + n_z - 1)
        send_whole(h, 0)
        send_whole(h, 1)

    @pl.loop(1, n_pa)
    def _(k):
        to_all(cbuf, c_s, c_r, k).start()

    def project_passage(k):
        load_p(k).wait()
        at = pl.ds(k * plen, plen)
        e = dot(ph[at, :], proj_ref[...])
        pe[at, :] = e
        u = (e * inverse_norm(e)).astype(BF16)
        pone[k, :, 0:vec] = u
        pone[k, :, vec:] = jnp.ones((plen, vec), BF16)
        pt[k] = u.astype(F32).T.astype(BF16)

    project_passage(0)

    @pl.loop(0, 2)
    def _(h):
        pass_on(h, 0)
        send_whole(h, 2)
        send_whole(h, 4)

    project_passage(1)

    @pl.loop(0, 2)
    def _(h):
        pass_on(h, 1)

    for k in range(2, n_p):
        project_passage(k)

    @pl.loop(0, 2)
    def _(h):
        finish(h, 0)
        send_whole(h, 3)

    narrow = lax.broadcasted_iota(jnp.int32, (8, 128), 1)

    @pl.loop(0, n_pa)
    def _(k):
        @pl.when(k == 1)
        def _():
            @pl.loop(0, 2)
            def _(h):
                pass_on(h, 2)
                pass_on(h, 4)

        @pl.when(k == 6)
        def _():
            @pl.loop(0, 2)
            def _(h):
                pass_on(h, 3)

        @pl.when(k == 9)
        def _():
            @pl.loop(0, 2)
            def _(h):
                finish(h, 1)

        @pl.when(k == 11)
        def _():
            @pl.loop(0, 2)
            def _(h):
                finish(h, 2)
                finish(h, 4)

        @pl.when(k == 15)
        def _():
            @pl.loop(0, 2)
            def _(h):
                finish(h, 3)

        dx, dy = pick(k, [d[0] for d in ORDER]), pick(k, [d[1] for d in ORDER])
        b = lax.rem(y + dy, SIDE) * SIDE + lax.rem(x + dx, SIDE)
        u = gq[b]
        at = pl.ds(pl.multiple_of(b * rows_q, rows_q), rows_q)
        for p in range(n_p):
            e = jnp.exp2(dot(u, pt[p]) * (LOG2E * scale)).astype(BF16)
            ex[p, at, :] = e
            sums = dot(e, pone[p])
            total = sums[:, vec:]
            inverse = 1.0 / total
            gn[p, at, :] = (sums[:, :vec] * inverse).astype(BF16)
            qn[p, at, :] = (u.astype(F32) * inverse).astype(BF16)
            four = total.reshape(queries, 4, qlen // 4, vec)
            logs = jnp.log((four[:, 0] * four[:, 1]) * (four[:, 2] * four[:, 3]))
            s = acc[p, b // 8]
            for i in range(queries):
                s = s + jnp.where(narrow == lax.rem(b, 8) * queries + i, logs[i], 0.0)
            acc[p, b // 8] = s

    for p in range(n_p):
        for i in range(2):
            score[me, p:p + 1, i * 128:(i + 1) * 128] = sharpness_divisor * jnp.sum(acc[p, i], axis=0, keepdims=True)

    @pl.loop(1, n_pa)
    def _(k):
        to_all(score, sc_s, sc_r, k).start()

    @pl.loop(1, n_pa)
    def _(k):
        from_all(cbuf, c_s, c_r, k).wait_recv()

    left, right = cbuf[0], cbuf[8]
    for i in range(1, 8):
        left = left + cbuf[i]
        right = right + cbuf[8 + i]
    named = jnp.concatenate([left, right], axis=1).astype(jnp.int32)
    rank = lax.broadcasted_iota(jnp.int32, (8, 256), 0)

    @pl.loop(0, n_pa)
    def _(o):
        ident = jnp.where(rank < n_p, o * n_p + rank, -1)
        first = (named[0:1, :] == ident).astype(F32)
        found = first
        for c in range(1, cand_count):
            found = found + (named[c:c + 1, :] == ident).astype(F32)
        mask[o] = found
        mark[o] = first

    @pl.loop(1, n_pa)
    def _(k):
        from_all(score, sc_s, sc_r, k).wait_recv()

    similarity = score[...]
    exponent = jnp.exp(similarity) * mask[...]
    element_total = jnp.sum(jnp.sum(exponent, axis=0), axis=0, keepdims=True)
    chosen = jnp.sum(jnp.sum(similarity * mark[...], axis=0), axis=0, keepdims=True)
    loss = jnp.log(element_total) - chosen
    mine_row = lax.broadcasted_iota(jnp.int32, (queries, 256), 1) == lax.broadcasted_iota(
        jnp.int32, (queries, 256), 0) + me * queries
    loss_ref[...] = jnp.broadcast_to(
        jnp.sum(jnp.where(mine_row, loss, 0.0), axis=1, keepdims=True), loss_ref.shape)
    grad_score = (jnp.exp(score[me]) * mask[me] / element_total - mark[me]) * (1.0 / vec)
    for p in range(n_p):
        gsrep[p] = jnp.broadcast_to(grad_score[p:p + 1, :], (vec, 256)).T

    q_half = queries // 2

    def spread(p, b, h, count):
        g = gsrep[p, pl.ds(pl.multiple_of(b * queries + h * q_half, 8), count), :]
        return jnp.broadcast_to(g[:, None, :], (count, qlen, vec)).reshape(count * qlen, vec)

    def value(h, g, o):
        if isinstance(g, int) and g == 0:
            return sum1[h * SIDE + o]
        b = slot(h, g - 1, o)
        at = pl.ds(pl.multiple_of(b * rows_q + h * hrow, hrow), hrow)
        result = spread(0, b, h, q_half) * gn[0, at, :].astype(F32)
        for p in range(1, n_p):
            result = result + spread(p, b, h, q_half) * gn[p, at, :].astype(F32)
        return result

    def leg1(h, g, k, to):
        i = h * 5 + g
        at = pl.ds(k * qrow, qrow)
        return remote(sbuf1.at[i, at], rbuf1.at[i, at], b_s.at[i * 4 + k], b_r.at[i * 4 + k], neighbour(h, g, to))

    def leg2(h, g, k, to):
        i = h * 5 + g
        return remote(sbuf2.at[i * 2 + k], rbuf2.at[i * 2 + k], b_s.at[i * 4 + 2 + k], b_r.at[i * 4 + 2 + k],
                      neighbour(h, g, to))

    def step1(h, g):
        sbuf1[h * 5 + g] = value(h, g, 2).astype(BF16)
        leg1(h, g, 0, 1).start()
        leg1(h, g, 1, 3).start()

    def step2(h, g):
        i = h * 5 + g
        v = value(h, g, 1)
        leg1(h, g, 0, 1).wait_recv()
        sbuf2[i * 2, 0:qrow, :] = (v[0:qrow] + rbuf1[i, 0:qrow, :].astype(F32)).astype(BF16)
        sbuf2[i * 2, qrow:, :] = v[qrow:].astype(BF16)
        leg2(h, g, 0, 1).start()
        v = value(h, g, 3)
        leg1(h, g, 1, 3).wait_recv()
        sbuf2[i * 2 + 1, 0:qrow, :] = v[0:qrow].astype(BF16)
        sbuf2[i * 2 + 1, qrow:, :] = (v[qrow:] + rbuf1[i, qrow:, :].astype(F32)).astype(BF16)
        leg2(h, g, 1, 3).start()

    def step3(h, g):
        i = h * 5 + g
        v = value(h, g, 0)
        leg2(h, g, 0, 1).wait_recv()
        v = v + rbuf2[i * 2].astype(F32)
        leg2(h, g, 1, 3).wait_recv()
        return v + rbuf2[i * 2 + 1].astype(F32)

    def grad_passage(first, last):
        @pl.loop(first, last)
        def _(b):
            at = pl.ds(pl.multiple_of(b * rows_q, rows_q), rows_q)
            for p in range(n_p):
                w = (spread(p, b, 0, queries) * qn[p, at, :].astype(F32)).astype(BF16)
                gp[p] += dot(ex[p, at, :], w, 0, 0)

    gp[...] = jnp.zeros_like(gp)

    @pl.loop(0, 8)
    def _(i):
        step1(i % 2, 1 + lax.rem(i // 2 + 2, SIDE))

    grad_passage(0, 3)

    @pl.loop(0, 8)
    def _(i):
        step2(i % 2, 1 + lax.rem(i // 2 + 2, SIDE))

    grad_passage(3, 9)

    @pl.loop(0, 2)
    def _(h):
        sum1[h * SIDE + 2] = step3(h, 3)
        step1(h, 0)

    grad_passage(9, 12)

    @pl.loop(0, 2)
    def _(h):
        sum1[h * SIDE + 1] = step3(h, 2)
        sum1[h * SIDE + 3] = step3(h, 4)
        sum1[h * SIDE] = step3(h, 1)
        step2(h, 0)

    grad_passage(12, 16)

    for p in range(n_p):
        at = pl.ds(p * plen, plen)
        g = norm_backward(pe[at, :], gp[p])
        pg_ref[at, :] = g
        pgb[at, :] = g.astype(BF16)

    quarter_rows = width // 8

    @pl.loop(0, 8)
    def _(c):
        at = pl.ds(pl.multiple_of(c * quarter_rows, quarter_rows), quarter_rows)
        wg[at, :] = dot(ph[:, at], pgb[...], 0, 0)

    for h in range(2):
        at = pl.ds(h * hrow, hrow)
        g = norm_backward(qe[at, :], step3(h, 0))
        qg_ref[at, :] = g
        qgb[at, :] = g.astype(BF16)

    half_rows = width // 2
    chunk = half_rows // n_pa
    piece = chunk // n_z
    base = core * half_rows

    def swap(j):
        at = pl.ds(pl.multiple_of(lax.rem(y + 1 + j, SIDE) * quarter_rows, quarter_rows), quarter_rows)
        return remote(half.at[at], got0.at[at], s0.at[j], r0.at[j], partner)

    def product(first, j):
        at = pl.ds(pl.multiple_of(first + lax.rem(y + 1 + j, SIDE) * quarter_rows, quarter_rows), quarter_rows)
        return wg[at, :] + dot(qh[:, at], qgb[...], 0, 0)

    @pl.loop(0, SIDE)
    def _(j):
        at = pl.ds(pl.multiple_of(lax.rem(y + 1 + j, SIDE) * quarter_rows, quarter_rows), quarter_rows)
        half[at, :] = product(half_rows - base, j).astype(BF16)
        swap(j).start()

    def to_xy(k, peer):
        return remote(part.at[peer], got1.at[me], s1.at[k], r1.at[n_pa - k], {"pa": peer})

    @pl.loop(0, SIDE)
    def _(j):
        v = product(base, j)
        row = lax.rem(y + 1 + j, SIDE)
        swap(j).wait_recv()
        v = v + got0[pl.ds(pl.multiple_of(row * quarter_rows, quarter_rows), quarter_rows), :].astype(F32)
        for i in range(SIDE):
            part[row * SIDE + i] = v[i * chunk:(i + 1) * chunk].astype(BF16)

            @pl.when((row == y) & (x == i))
            def _():
                mine[...] = v[i * chunk:(i + 1) * chunk]

        @pl.loop(1, SIDE + 1)
        def _(i):
            peer = row * SIDE + lax.rem(x + i, SIDE)

            @pl.when(peer != me)
            def _():
                to_xy(lax.rem(peer + n_pa - me, n_pa), peer).start()

    @pl.loop(1, n_pa)
    def _(k):
        remote(part.at[xy(k)], got1.at[xy(k)], s1.at[k], r1.at[k], {"pa": xy(k)}).wait_recv()
        mine[...] += got1[xy(k)].astype(F32)

    part[me] = mine[...].astype(BF16)

    def to_z(k):
        return remote(part.at[me, pl.ds(zz(k) * piece, piece)], got2.at[z], s2.at[k],
                      r2.at[n_z - k], {"pb": zz(k) * 2 + core})

    @pl.loop(1, n_z)
    def _(k):
        to_z(k).start()

    total = mine[pl.ds(z * piece, piece), :]
    for k in range(1, n_z):
        remote(got2.at[zz(k)], got2.at[zz(k)], s2.at[k], r2.at[k], {"pb": zz(k) * 2 + core}).wait_recv()
        total = total + got2[zz(k)].astype(F32)

    out[pl.ds(base + me * chunk + z * piece, piece), :] = total.astype(BF16)

    def back_z(k, who, recv):
        at = pl.ds(base + me * chunk + who * piece, piece)
        return remote(out.at[at], out.at[at], s3.at[k], r3.at[recv], {"pb": zz(k) * 2 + core})

    @pl.loop(1, n_z)
    def _(k):
        back_z(k, z, n_z - k).start()

    @pl.loop(1, n_z)
    def _(k):
        back_z(k, zz(k), k).wait_recv()

    def back_xy(k, who, recv):
        at = pl.ds(base + who * chunk, chunk)
        return remote(out.at[at], out.at[at], s4.at[k], r4.at[recv], {"pa": xy(k)})

    @pl.loop(1, n_pa)
    def _(k):
        back_xy(k, me, n_pa - k).start()

    def across(k, first):
        at = pl.ds(first + xy(k) * chunk, chunk)
        return remote(out.at[at], out.at[at], s5.at[k], r5.at[k], partner)

    across(0, base).start()

    @pl.loop(1, n_pa)
    def _(k):
        back_xy(k, xy(k), k).wait_recv()
        across(k, base).start()

    @pl.loop(0, n_pa)
    def _(k):
        across(k, half_rows - base).wait_recv()

    wg_ref[...] = out[...]

    @pl.loop(0, 10)
    def _(i):
        h, g = i // 5, lax.rem(i, 5)
        sent(h, g)
        leg1(h, g, 0, 1).wait_send()
        leg1(h, g, 1, 3).wait_send()
        leg2(h, g, 0, 1).wait_send()
        leg2(h, g, 1, 3).wait_send()

    @pl.loop(1, n_pa)
    def _(k):
        to_all(cbuf, c_s, c_r, k).wait_send()
        to_all(score, sc_s, sc_r, k).wait_send()
        to_xy(k, xy(k)).wait_send()
        back_xy(k, me, n_pa - k).wait_send()

    @pl.loop(1, n_z)
    def _(k):
        to_z(k).wait_send()
        back_z(k, z, n_z - k).wait_send()

    @pl.loop(0, SIDE)
    def _(j):
        swap(j).wait_send()

    @pl.loop(0, n_pa)
    def _(k):
        across(k, base).wait_send()


def shards(query_hidden, passage_hidden, projection, candidates):
    queries, qlen, width = query_hidden.shape
    n_p, plen, _ = passage_hidden.shape
    vec = projection.shape[1]
    n_pa, n_z = lax.axis_size("pa"), lax.axis_size("pb") // 2
    rows_q, rows_p = queries * qlen, n_p * plen
    all_rows = n_pa * rows_q
    hrow = rows_q // 2
    half_rows = width // 2
    chunk = half_rows // n_pa
    piece = chunk // n_z
    cand = jnp.pad(candidates.T.astype(F32), ((0, 16 - candidates.shape[1]), (0, 128 - queries)))
    dma = pltpu.SemaphoreType.DMA
    V = pltpu.VMEM
    in_vmem, anywhere = pl.BlockSpec(memory_space=pltpu.VMEM), pl.BlockSpec(memory_space=pl.ANY)
    loss, query_grad, passage_grad, weight_grad = pl.pallas_call(
        functools.partial(kernel, n_z, qlen, candidates.shape[1]),
        out_shape=(
            jax.ShapeDtypeStruct((queries, 128), F32),
            jax.ShapeDtypeStruct((rows_q, vec), F32),
            jax.ShapeDtypeStruct((rows_p, vec), F32),
            jax.ShapeDtypeStruct((width, vec), BF16),
        ),
        in_specs=[anywhere, anywhere, in_vmem, in_vmem],
        out_specs=(in_vmem,) * 4,
        scratch_shapes=[
            V((rows_q, width), BF16), V((rows_p, width), BF16), V((rows_q, vec), F32), V((rows_p, vec), F32),
            V((n_p, vec, plen), BF16), V((n_p, plen, 2 * vec), BF16), V((n_pa, rows_q, vec), BF16),
            V((n_p, all_rows, plen), BF16), V((n_p, all_rows, vec), BF16), V((n_p, all_rows, vec), BF16),
            V((n_p, 2, 8, 128), F32), V((n_pa, 16, 128), F32), V((n_pa, 8, 256), F32), V((n_pa, 8, 256), F32),
            V((n_pa, 8, 256), F32), V((n_p, 256, vec), F32),
            V((10, hrow, vec), BF16), V((20, hrow, vec), BF16), V((10, hrow, vec), BF16), V((20, hrow, vec), BF16),
            V((2 * SIDE, hrow, vec), F32), V((n_p, plen, vec), F32), V((rows_q, vec), BF16), V((rows_p, vec), BF16),
            V((width, vec), F32), V((width, vec), BF16), V((half_rows, vec), BF16), V((half_rows, vec), BF16),
            V((n_pa, chunk, vec), BF16), V((n_pa, chunk, vec), BF16), V((chunk, vec), F32), V((n_z, piece, vec), BF16),
            dma((2 + n_p,)), dma((n_pa,)), dma((n_pa,)), dma((n_pa,)), dma((n_pa,)),
            dma((40,)), dma((40,)), dma((40,)), dma((40,)),
            dma((SIDE,)), dma((SIDE,)), dma((n_pa,)), dma((n_pa,)), dma((n_z,)), dma((n_z,)),
            dma((n_z,)), dma((n_z,)), dma((n_pa,)), dma((n_pa,)), dma((n_pa,)), dma((n_pa,)),
        ],
        compiler_params=pltpu.CompilerParams(collective_id=0, has_side_effects=True, vmem_limit_bytes=60 * 2**20),
        name="retriever",
    )(query_hidden.reshape(rows_q, width), passage_hidden.reshape(rows_p, width), projection, cand)
    return (
        loss[:, 0],
        query_grad.reshape(queries, qlen, vec),
        passage_grad.reshape(n_p, plen, vec),
        weight_grad.astype(F32),
    )


def solution(mesh):
    placed = (P(("pb", "pa"), None, None), P(("pb", "pa"), None, None), P(), P(("pb", "pa"), None))
    return jax.shard_map(
        shards,
        mesh=mesh,
        in_specs=placed,
        out_specs=(P(("pb", "pa")), P(("pb", "pa"), None, None), P(("pb", "pa"), None, None), P()),
        check_vma=False,
    )
```

```python
import functools
import jax
import jax.numpy as jnp
from jax import lax
from jax.experimental import pallas as pl
from jax.experimental.pallas import tpu as pltpu
from jax.sharding import PartitionSpec as P

MESH = pl.DeviceIdType.MESH
F32, BF16 = jnp.float32, jnp.bfloat16
SIDE = 4
sharpness_divisor = 0.1
epsilon = 1e-06
LOG2E = 1.4426950408889634


def remote(src, dst, send, recv, device):
    return pltpu.make_async_remote_copy(
        src_ref=src, dst_ref=dst, send_sem=send, recv_sem=recv, device_id=device, device_id_type=MESH
    )


def dot(a, b, ca=1, cb=0):
    return lax.dot_general(a, b, (((ca,), (cb,)), ((), ())), preferred_element_type=F32)


def inverse_norm(embedded):
    return lax.rsqrt(jnp.mean(embedded * embedded, axis=-1, keepdims=True) + epsilon)


def norm_backward(embedded, unit_grad):
    inv_norm = inverse_norm(embedded)
    inner_mean = jnp.mean(embedded * unit_grad, axis=-1, keepdims=True)
    return inv_norm * unit_grad - inv_norm * inv_norm * inv_norm * embedded * inner_mean


def pick(k, values):
    result = jnp.int32(values[0])
    for i, v in enumerate(values[1:]):
        result = jnp.where(k == i + 1, jnp.int32(v), result)
    return result


ORDER = [(0, 0), (1, 0), (3, 0), (0, 1), (0, 3), (1, 1), (1, 3), (3, 1), (3, 3),
         (2, 0), (0, 2), (2, 1), (2, 3), (1, 2), (3, 2), (2, 2)]


def kernel(n_z, qlen, cand_count,
           qh_ref, ph_ref, proj_ref, cand_ref,
           loss_ref, qg_ref, pg_ref, wg_ref,
           qh, ph, qe, pe, pt, pone, gq, ex, gn, qn, acc, cbuf, mask, mark, score, gsrep,
           sbuf1, sbuf2, rbuf1, rbuf2, sum1, gp, qgb, pgb,
           wg, out, half, got0, part, got1, mine, got2,
           sem_h, c_s, c_r, sc_s, sc_r, a_s, a_r, b_s, b_r,
           s0, r0, s1, r1, s2, r2, s4, r4, s5, r5):
    n_pa = SIDE * SIDE
    rows_q = qh.shape[0]
    hrow = rows_q // 2
    qrow = hrow // 2
    queries = rows_q // qlen
    n_p, plen = pone.shape[0], pone.shape[1]
    width = qh.shape[1]
    vec = proj_ref.shape[1]
    me, pb = lax.axis_index("pa"), lax.axis_index("pb")
    y, x = me // SIDE, me % SIDE
    z, core = pb // 2, pb % 2
    partner = {"pb": z * 2 + (1 - core)}
    scale = 1.0 / (vec * sharpness_divisor)

    def xy(k):
        return lax.rem(me + k, n_pa)

    def zz(k):
        return lax.rem(z + k, n_z)

    def load_q(k):
        at = pl.ds(k * hrow, hrow)
        return pltpu.make_async_copy(qh_ref.at[at], qh.at[at], sem_h.at[k])

    def load_p(k):
        at = pl.ds(k * plen, plen)
        return pltpu.make_async_copy(ph_ref.at[at], ph.at[at], sem_h.at[2 + k])

    for k in range(2):
        load_q(k).start()
    for k in range(n_p):
        load_p(k).start()

    barrier = pltpu.get_barrier_semaphore()
    pl.semaphore_signal(barrier, inc=1, device_id=partner, device_id_type=MESH)

    @pl.loop(1, n_pa)
    def _(k):
        pl.semaphore_signal(barrier, inc=1, device_id={"pa": xy(k)}, device_id_type=MESH)

    @pl.loop(1, n_z)
    def _(k):
        pl.semaphore_signal(barrier, inc=1, device_id={"pb": zz(k) * 2 + core}, device_id_type=MESH)

    lane = lax.broadcasted_iota(jnp.int32, (queries, 128), 1)
    line = lax.broadcasted_iota(jnp.int32, (queries, 128), 0)
    place = (lane == line + (me % 8) * queries).astype(F32)
    cbuf[me] = jnp.zeros((16, 128), F32)
    cbuf[me, 0:cand_count, :] = dot(cand_ref[...].astype(F32), place, 0, 0)
    score[...] = jnp.zeros_like(score)
    acc[...] = jnp.zeros_like(acc)

    def slot(h, d1, d2):
        dx, dy = d1 * (1 - h) + d2 * h, d2 * (1 - h) + d1 * h
        return lax.rem(y + dy, SIDE) * SIDE + lax.rem(x + dx, SIDE)

    def offset(h, g, o):
        first = jnp.int32(g == 0) if isinstance(g, int) else (g == 0).astype(jnp.int32)
        d1 = first * o + (1 - first) * (g - 1)
        return d1, (1 - first) * o

    def neighbour(h, g, o):
        first = jnp.int32(g == 0) if isinstance(g, int) else (g == 0).astype(jnp.int32)
        return {"pa": slot(h, first * o, (1 - first) * o)}

    def whole(h, g, o, k, to):
        block = gq.at[slot(h, *offset(h, g, o)), pl.ds(h * hrow, hrow)]
        i = (h * 5 + g) * 4 + k
        return remote(block, block, a_s.at[i], a_r.at[i], neighbour(h, g, to))

    def quarter(h, g, o, k, to):
        block = gq.at[slot(h, *offset(h, g, o)), pl.ds(h * hrow + (k - 2) * qrow, qrow)]
        i = (h * 5 + g) * 4 + k
        return remote(block, block, a_s.at[i], a_r.at[i], neighbour(h, g, to))

    def send_whole(h, g):
        whole(h, g, 0, 0, 1).start()
        whole(h, g, 0, 1, 3).start()

    def pass_on(h, g):
        whole(h, g, 3, 0, 1).wait_recv()
        quarter(h, g, 3, 2, 1).start()
        whole(h, g, 1, 1, 3).wait_recv()
        quarter(h, g, 1, 3, 3).start()

    def finish(h, g):
        quarter(h, g, 2, 2, 1).wait_recv()
        quarter(h, g, 2, 3, 3).wait_recv()

    def sent(h, g):
        whole(h, g, 0, 0, 1).wait_send()
        whole(h, g, 0, 1, 3).wait_send()
        quarter(h, g, 3, 2, 1).wait_send()
        quarter(h, g, 1, 3, 3).wait_send()

    def to_all(buf, send, recv, k):
        return remote(buf.at[me], buf.at[me], send.at[k], recv.at[n_pa - k], {"pa": xy(k)})

    def from_all(buf, send, recv, k):
        return remote(buf.at[xy(k)], buf.at[xy(k)], send.at[k], recv.at[k], {"pa": xy(k)})

    for h in range(2):
        at = pl.ds(h * hrow, hrow)
        load_q(h).wait()
        e = dot(qh[at, :], proj_ref[...])
        qe[at, :] = e
        gq[me, at, :] = (e * inverse_norm(e)).astype(BF16)
        if h == 0:
            pl.semaphore_wait(barrier, n_pa + n_z - 1)
        send_whole(h, 0)
        send_whole(h, 1)

    @pl.loop(1, n_pa)
    def _(k):
        to_all(cbuf, c_s, c_r, k).start()

    def project_passage(k):
        load_p(k).wait()
        at = pl.ds(k * plen, plen)
        e = dot(ph[at, :], proj_ref[...])
        pe[at, :] = e
        u = (e * inverse_norm(e)).astype(BF16)
        pone[k, :, 0:vec] = u
        pone[k, :, vec:] = jnp.ones((plen, vec), BF16)
        pt[k] = u.astype(F32).T.astype(BF16)

    project_passage(0)

    @pl.loop(0, 2)
    def _(h):
        pass_on(h, 0)
        send_whole(h, 2)
        send_whole(h, 4)

    project_passage(1)

    @pl.loop(0, 2)
    def _(h):
        pass_on(h, 1)

    for k in range(2, n_p):
        project_passage(k)

    narrow = lax.broadcasted_iota(jnp.int32, (8, 128), 1)

    @pl.loop(0, n_pa)
    def _(k):
        @pl.when(k == 2)
        def _():
            @pl.loop(0, 2)
            def _(h):
                finish(h, 0)
                send_whole(h, 3)

        @pl.when(k == 4)
        def _():
            @pl.loop(0, 2)
            def _(h):
                pass_on(h, 2)
                pass_on(h, 4)

        @pl.when(k == 7)
        def _():
            @pl.loop(0, 2)
            def _(h):
                pass_on(h, 3)

        @pl.when(k == 9)
        def _():
            @pl.loop(0, 2)
            def _(h):
                finish(h, 1)

        @pl.when(k == 11)
        def _():
            @pl.loop(0, 2)
            def _(h):
                finish(h, 2)
                finish(h, 4)

        @pl.when(k == 15)
        def _():
            @pl.loop(0, 2)
            def _(h):
                finish(h, 3)

        dx, dy = pick(k, [d[0] for d in ORDER]), pick(k, [d[1] for d in ORDER])
        b = lax.rem(y + dy, SIDE) * SIDE + lax.rem(x + dx, SIDE)
        u = gq[b]
        at = pl.ds(pl.multiple_of(b * rows_q, rows_q), rows_q)
        for p in range(n_p):
            e = jnp.exp2(dot(u, pt[p]) * (LOG2E * scale)).astype(BF16)
            ex[p, at, :] = e
            sums = dot(e, pone[p])
            total = sums[:, vec:]
            inverse = 1.0 / total
            gn[p, at, :] = (sums[:, :vec] * inverse).astype(BF16)
            qn[p, at, :] = (u.astype(F32) * inverse).astype(BF16)
            four = total.reshape(queries, 4, qlen // 4, vec)
            logs = jnp.log((four[:, 0] * four[:, 1]) * (four[:, 2] * four[:, 3]))
            s = acc[p, b // 8]
            for i in range(queries):
                s = s + jnp.where(narrow == lax.rem(b, 8) * queries + i, logs[i], 0.0)
            acc[p, b // 8] = s

    for p in range(n_p):
        for i in range(2):
            score[me, p:p + 1, i * 128:(i + 1) * 128] = sharpness_divisor * jnp.sum(acc[p, i], axis=0, keepdims=True)

    @pl.loop(1, n_pa)
    def _(k):
        to_all(score, sc_s, sc_r, k).start()

    @pl.loop(1, n_pa)
    def _(k):
        from_all(cbuf, c_s, c_r, k).wait_recv()

    left, right = cbuf[0], cbuf[8]
    for i in range(1, 8):
        left = left + cbuf[i]
        right = right + cbuf[8 + i]
    named = jnp.concatenate([left, right], axis=1).astype(jnp.int32)
    rank = lax.broadcasted_iota(jnp.int32, (8, 256), 0)

    @pl.loop(0, n_pa)
    def _(o):
        ident = jnp.where(rank < n_p, o * n_p + rank, -1)
        first = (named[0:1, :] == ident).astype(F32)
        found = first
        for c in range(1, cand_count):
            found = found + (named[c:c + 1, :] == ident).astype(F32)
        mask[o] = found
        mark[o] = first

    @pl.loop(1, n_pa)
    def _(k):
        from_all(score, sc_s, sc_r, k).wait_recv()

    similarity = score[...]
    exponent = jnp.exp(similarity) * mask[...]
    element_total = jnp.sum(jnp.sum(exponent, axis=0), axis=0, keepdims=True)
    chosen = jnp.sum(jnp.sum(similarity * mark[...], axis=0), axis=0, keepdims=True)
    loss = jnp.log(element_total) - chosen
    mine_row = lax.broadcasted_iota(jnp.int32, (queries, 256), 1) == lax.broadcasted_iota(
        jnp.int32, (queries, 256), 0) + me * queries
    column = jnp.sum(jnp.where(mine_row, loss, 0.0), axis=1, keepdims=True)
    loss_ref[...] = jnp.sum(jnp.where(lane == line, column, 0.0), axis=0, keepdims=True)
    grad_score = (jnp.exp(score[me]) * mask[me] / element_total - mark[me]) * (1.0 / vec)
    for p in range(n_p):
        gsrep[p] = jnp.broadcast_to(grad_score[p:p + 1, :], (vec, 256)).T

    q_half = queries // 2

    def spread(p, b, h, count):
        g = gsrep[p, pl.ds(pl.multiple_of(b * queries + h * q_half, 8), count), :]
        return jnp.broadcast_to(g[:, None, :], (count, qlen, vec)).reshape(count * qlen, vec)

    def value(h, g, o):
        if isinstance(g, int) and g == 0:
            return sum1[h * SIDE + o]
        b = slot(h, g - 1, o)
        at = pl.ds(pl.multiple_of(b * rows_q + h * hrow, hrow), hrow)
        result = spread(0, b, h, q_half) * gn[0, at, :].astype(F32)
        for p in range(1, n_p):
            result = result + spread(p, b, h, q_half) * gn[p, at, :].astype(F32)
        return result

    def leg1(h, g, k, to):
        i = h * 5 + g
        at = pl.ds(k * qrow, qrow)
        return remote(sbuf1.at[i, at], rbuf1.at[i, at], b_s.at[i * 4 + k], b_r.at[i * 4 + k], neighbour(h, g, to))

    def leg2(h, g, k, to):
        i = h * 5 + g
        return remote(sbuf2.at[i * 2 + k], rbuf2.at[i * 2 + k], b_s.at[i * 4 + 2 + k], b_r.at[i * 4 + 2 + k],
                      neighbour(h, g, to))

    def step1(h, g):
        sbuf1[h * 5 + g] = value(h, g, 2).astype(BF16)
        leg1(h, g, 0, 1).start()
        leg1(h, g, 1, 3).start()

    def step2(h, g):
        i = h * 5 + g
        v = value(h, g, 1)
        leg1(h, g, 0, 1).wait_recv()
        sbuf2[i * 2, 0:qrow, :] = (v[0:qrow] + rbuf1[i, 0:qrow, :].astype(F32)).astype(BF16)
        sbuf2[i * 2, qrow:, :] = v[qrow:].astype(BF16)
        leg2(h, g, 0, 1).start()
        v = value(h, g, 3)
        leg1(h, g, 1, 3).wait_recv()
        sbuf2[i * 2 + 1, 0:qrow, :] = v[0:qrow].astype(BF16)
        sbuf2[i * 2 + 1, qrow:, :] = (v[qrow:] + rbuf1[i, qrow:, :].astype(F32)).astype(BF16)
        leg2(h, g, 1, 3).start()

    def step3(h, g):
        i = h * 5 + g
        v = value(h, g, 0)
        leg2(h, g, 0, 1).wait_recv()
        v = v + rbuf2[i * 2].astype(F32)
        leg2(h, g, 1, 3).wait_recv()
        return v + rbuf2[i * 2 + 1].astype(F32)

    def grad_passage(first, last):
        @pl.loop(first, last)
        def _(b):
            at = pl.ds(pl.multiple_of(b * rows_q, rows_q), rows_q)
            for p in range(n_p):
                w = (spread(p, b, 0, queries) * qn[p, at, :].astype(F32)).astype(BF16)
                gp[p] += dot(ex[p, at, :], w, 0, 0)

    gp[...] = jnp.zeros_like(gp)

    @pl.loop(0, 8)
    def _(i):
        step1(i % 2, 1 + lax.rem(i // 2 + 2, SIDE))

    grad_passage(0, 3)

    @pl.loop(0, 8)
    def _(i):
        step2(i % 2, 1 + lax.rem(i // 2 + 2, SIDE))

    grad_passage(3, 9)

    @pl.loop(0, 2)
    def _(h):
        sum1[h * SIDE + 2] = step3(h, 3)
        step1(h, 0)

    grad_passage(9, 12)

    @pl.loop(0, 2)
    def _(h):
        sum1[h * SIDE + 1] = step3(h, 2)
        sum1[h * SIDE + 3] = step3(h, 4)
        sum1[h * SIDE] = step3(h, 1)
        step2(h, 0)

    grad_passage(12, 16)

    for p in range(n_p):
        at = pl.ds(p * plen, plen)
        g = norm_backward(pe[at, :], gp[p])
        pg_ref[at, :] = g
        pgb[at, :] = g.astype(BF16)

    quarter_rows = width // 8

    @pl.loop(0, 8)
    def _(c):
        at = pl.ds(pl.multiple_of(c * quarter_rows, quarter_rows), quarter_rows)
        wg[at, :] = dot(ph[:, at], pgb[...], 0, 0)

    for h in range(2):
        at = pl.ds(h * hrow, hrow)
        g = norm_backward(qe[at, :], step3(h, 0))
        qg_ref[at, :] = g
        qgb[at, :] = g.astype(BF16)

    half_rows = width // 2
    chunk = half_rows // n_pa
    base = core * half_rows

    def swap(j):
        at = pl.ds(pl.multiple_of(lax.rem(y + 1 + j, SIDE) * quarter_rows, quarter_rows), quarter_rows)
        return remote(half.at[at], got0.at[at], s0.at[j], r0.at[j], partner)

    def product(first, j):
        at = pl.ds(pl.multiple_of(first + lax.rem(y + 1 + j, SIDE) * quarter_rows, quarter_rows), quarter_rows)
        return wg[at, :] + dot(qh[:, at], qgb[...], 0, 0)

    @pl.loop(0, SIDE)
    def _(j):
        at = pl.ds(pl.multiple_of(lax.rem(y + 1 + j, SIDE) * quarter_rows, quarter_rows), quarter_rows)
        half[at, :] = product(half_rows - base, j).astype(BF16)
        swap(j).start()

    def to_xy(k, peer):
        return remote(part.at[peer], got1.at[me], s1.at[k], r1.at[n_pa - k], {"pa": peer})

    @pl.loop(0, SIDE)
    def _(j):
        v = product(base, j)
        row = lax.rem(y + 1 + j, SIDE)
        swap(j).wait_recv()
        v = v + got0[pl.ds(pl.multiple_of(row * quarter_rows, quarter_rows), quarter_rows), :].astype(F32)
        for i in range(SIDE):
            part[row * SIDE + i] = v[i * chunk:(i + 1) * chunk].astype(BF16)

            @pl.when((row == y) & (x == i))
            def _():
                mine[...] = v[i * chunk:(i + 1) * chunk]

        @pl.loop(1, SIDE + 1)
        def _(i):
            peer = row * SIDE + lax.rem(x + i, SIDE)

            @pl.when(peer != me)
            def _():
                to_xy(lax.rem(peer + n_pa - me, n_pa), peer).start()

    @pl.loop(1, n_pa)
    def _(k):
        remote(part.at[xy(k)], got1.at[xy(k)], s1.at[k], r1.at[k], {"pa": xy(k)}).wait_recv()
        mine[...] += got1[xy(k)].astype(F32)

    part[me] = mine[...].astype(BF16)
    got2[z] = mine[...].astype(BF16)

    def to_z(k, who, recv):
        return remote(part.at[me], got2.at[who], s2.at[k], r2.at[recv], {"pb": zz(k) * 2 + core})

    @pl.loop(1, n_z)
    def _(k):
        to_z(k, z, n_z - k).start()

    @pl.loop(1, n_z)
    def _(k):
        to_z(k, zz(k), k).wait_recv()

    total = got2[0].astype(F32)
    for k in range(1, n_z):
        total = total + got2[k].astype(F32)
    out[pl.ds(base + me * chunk, chunk), :] = total.astype(BF16)

    def back_xy(k, who, recv):
        at = pl.ds(base + who * chunk, chunk)
        return remote(out.at[at], out.at[at], s4.at[k], r4.at[recv], {"pa": xy(k)})

    @pl.loop(1, n_pa)
    def _(k):
        back_xy(k, me, n_pa - k).start()

    def across(k, first):
        at = pl.ds(first + xy(k) * chunk, chunk)
        return remote(out.at[at], out.at[at], s5.at[k], r5.at[k], partner)

    across(0, base).start()

    @pl.loop(1, n_pa)
    def _(k):
        back_xy(k, xy(k), k).wait_recv()
        across(k, base).start()

    @pl.loop(0, n_pa)
    def _(k):
        across(k, half_rows - base).wait_recv()

    wg_ref[...] = out[...]

    @pl.loop(0, 10)
    def _(i):
        h, g = i // 5, lax.rem(i, 5)
        sent(h, g)
        leg1(h, g, 0, 1).wait_send()
        leg1(h, g, 1, 3).wait_send()
        leg2(h, g, 0, 1).wait_send()
        leg2(h, g, 1, 3).wait_send()

    @pl.loop(1, n_pa)
    def _(k):
        to_all(cbuf, c_s, c_r, k).wait_send()
        to_all(score, sc_s, sc_r, k).wait_send()
        to_xy(k, xy(k)).wait_send()
        back_xy(k, me, n_pa - k).wait_send()

    @pl.loop(1, n_z)
    def _(k):
        to_z(k, z, n_z - k).wait_send()

    @pl.loop(0, SIDE)
    def _(j):
        swap(j).wait_send()

    @pl.loop(0, n_pa)
    def _(k):
        across(k, base).wait_send()


def hand_over(loss_ref, qg_ref, pg_ref, wg_ref, loss_out, qg_out, pg_out, wg_out):
    loss_out[...] = loss_ref[:, 0:loss_out.shape[1]]
    qg_out[...] = qg_ref[...]
    pg_out[...] = pg_ref[...]
    wg_out[...] = wg_ref[...].astype(F32)


def shards(query_hidden, passage_hidden, projection, candidates):
    queries, qlen, width = query_hidden.shape
    n_p, plen, _ = passage_hidden.shape
    vec = projection.shape[1]
    n_pa, n_z = lax.axis_size("pa"), lax.axis_size("pb") // 2
    rows_q, rows_p = queries * qlen, n_p * plen
    all_rows = n_pa * rows_q
    hrow = rows_q // 2
    half_rows = width // 2
    chunk = half_rows // n_pa
    dma = pltpu.SemaphoreType.DMA
    V = pltpu.VMEM
    in_vmem, anywhere = pl.BlockSpec(memory_space=pltpu.VMEM), pl.BlockSpec(memory_space=pl.ANY)
    loss, query_grad, passage_grad, weight_grad = pl.pallas_call(
        functools.partial(kernel, n_z, qlen, candidates.shape[1]),
        out_shape=(
            jax.ShapeDtypeStruct((1, 128), F32),
            jax.ShapeDtypeStruct((rows_q, vec), F32),
            jax.ShapeDtypeStruct((rows_p, vec), F32),
            jax.ShapeDtypeStruct((width, vec), BF16),
        ),
        in_specs=[anywhere, anywhere, in_vmem, in_vmem],
        out_specs=(in_vmem,) * 4,
        scratch_shapes=[
            V((rows_q, width), BF16), V((rows_p, width), BF16), V((rows_q, vec), F32), V((rows_p, vec), F32),
            V((n_p, vec, plen), BF16), V((n_p, plen, 2 * vec), BF16), V((n_pa, rows_q, vec), BF16),
            V((n_p, all_rows, plen), BF16), V((n_p, all_rows, vec), BF16), V((n_p, all_rows, vec), BF16),
            V((n_p, 2, 8, 128), F32), V((n_pa, 16, 128), F32), V((n_pa, 8, 256), F32), V((n_pa, 8, 256), F32),
            V((n_pa, 8, 256), F32), V((n_p, 256, vec), F32),
            V((10, hrow, vec), BF16), V((20, hrow, vec), BF16), V((10, hrow, vec), BF16), V((20, hrow, vec), BF16),
            V((2 * SIDE, hrow, vec), F32), V((n_p, plen, vec), F32), V((rows_q, vec), BF16), V((rows_p, vec), BF16),
            V((width, vec), F32), V((width, vec), BF16), V((half_rows, vec), BF16), V((half_rows, vec), BF16),
            V((n_pa, chunk, vec), BF16), V((n_pa, chunk, vec), BF16), V((chunk, vec), F32), V((n_z, chunk, vec), BF16),
            dma((2 + n_p,)), dma((n_pa,)), dma((n_pa,)), dma((n_pa,)), dma((n_pa,)),
            dma((40,)), dma((40,)), dma((40,)), dma((40,)),
            dma((SIDE,)), dma((SIDE,)), dma((n_pa,)), dma((n_pa,)), dma((n_z,)), dma((n_z,)),
            dma((n_pa,)), dma((n_pa,)), dma((n_pa,)), dma((n_pa,)),
        ],
        compiler_params=pltpu.CompilerParams(collective_id=0, has_side_effects=True, vmem_limit_bytes=60 * 2**20),
        name="retriever",
    )(query_hidden.reshape(rows_q, width), passage_hidden.reshape(rows_p, width), projection, candidates)
    loss, query_grad, passage_grad, weight_grad = pl.pallas_call(
        hand_over,
        out_shape=(
            jax.ShapeDtypeStruct((1, queries), F32),
            jax.ShapeDtypeStruct((rows_q, vec), F32),
            jax.ShapeDtypeStruct((rows_p, vec), F32),
            jax.ShapeDtypeStruct((width, vec), F32),
        ),
        in_specs=[in_vmem] * 4,
        out_specs=(in_vmem,) * 4,
        name="hand_over",
    )(loss, query_grad, passage_grad, weight_grad)
    return (
        loss.reshape(queries),
        query_grad.reshape(queries, qlen, vec),
        passage_grad.reshape(n_p, plen, vec),
        weight_grad,
    )


def solution(mesh):
    placed = (P(("pb", "pa"), None, None), P(("pb", "pa"), None, None), P(), P(("pb", "pa"), None))
    return jax.shard_map(
        shards,
        mesh=mesh,
        in_specs=placed,
        out_specs=(P(("pb", "pa")), P(("pb", "pa"), None, None), P(("pb", "pa"), None, None), P()),
        check_vma=False,
    )
```

```python
import functools
import jax
import jax.numpy as jnp
from jax import lax
from jax.experimental import pallas as pl
from jax.experimental.pallas import tpu as pltpu
from jax.sharding import PartitionSpec as P

MESH = pl.DeviceIdType.MESH
F32, BF16 = jnp.float32, jnp.bfloat16
SIDE = 4
sharpness_divisor = 0.1
epsilon = 1e-06
LOG2E = 1.4426950408889634


def remote(src, dst, send, recv, device):
    return pltpu.make_async_remote_copy(
        src_ref=src, dst_ref=dst, send_sem=send, recv_sem=recv, device_id=device, device_id_type=MESH
    )


def dot(a, b, ca=1, cb=0):
    return lax.dot_general(a, b, (((ca,), (cb,)), ((), ())), preferred_element_type=F32)


def inverse_norm(embedded):
    return lax.rsqrt(jnp.mean(embedded * embedded, axis=-1, keepdims=True) + epsilon)


def norm_backward(embedded, unit_grad):
    inv_norm = inverse_norm(embedded)
    inner_mean = jnp.mean(embedded * unit_grad, axis=-1, keepdims=True)
    return inv_norm * unit_grad - inv_norm * inv_norm * inv_norm * embedded * inner_mean


def pick(k, values):
    result = values[0]
    for i, v in enumerate(values[1:]):
        result = jnp.where(k == i + 1, v, result)
    return result


FAR = [10, 9, 11, 6, 14, 2, 8, 5, 7, 13, 15, 1, 3, 4, 12]
ORDER = [(0, 0), (1, 0), (3, 0), (0, 1), (0, 3), (1, 1), (1, 3), (3, 1), (3, 3),
         (2, 0), (0, 2), (2, 1), (2, 3), (1, 2), (3, 2), (2, 2)]


def kernel(n_z, qlen, cand_count,
           qh_ref, ph_ref, proj_ref, cand_ref,
           loss_ref, qg_ref, pg_ref, wg_ref,
           proj, qh, ph, qe, pe, pt, pone, gq, ex, gn, qn, acc, cbuf, mask, mark, score, gsrep,
           sbuf1, sbuf2, rbuf1, rbuf2, sum1, gp, qgb, pgb,
           wg, out, half, got0, part, got1, mine, got2,
           sem_h, c_s, c_r, sc_s, sc_r, a_s, a_r, b_s, b_r,
           s0, r0, s1, r1, s2, r2, s4, r4, s5, r5):
    n_pa = SIDE * SIDE
    rows_q = qh.shape[0]
    hrow = rows_q // 2
    qrow = hrow // 2
    queries = rows_q // qlen
    n_p, plen = pone.shape[0], pone.shape[1]
    width = qh.shape[1]
    vec = proj.shape[1]
    me, pb = lax.axis_index("pa"), lax.axis_index("pb")
    y, x = me // SIDE, me % SIDE
    z, core = pb // 2, pb % 2
    partner = {"pb": z * 2 + (1 - core)}
    scale = 1.0 / (vec * sharpness_divisor)

    rows = [lax.rem(y + d, SIDE) * SIDE for d in range(SIDE)]
    columns = [lax.rem(x + d, SIDE) for d in range(SIDE)]
    at_offset = [rows[k // SIDE] + columns[k % SIDE] for k in range(n_pa)]
    along_z = [lax.rem(z + k, n_z) for k in range(n_z)]

    def back(k):
        return (SIDE - k // SIDE) % SIDE * SIDE + (SIDE - k % SIDE) % SIDE

    def plane(k):
        return {"pa": at_offset[k]}

    def line_z(k):
        return {"pb": along_z[k] * 2 + core}

    def load_q(k):
        at = pl.ds(k * hrow, hrow)
        return pltpu.make_async_copy(qh_ref.at[at], qh.at[at], sem_h.at[k])

    def load_p(k):
        at = pl.ds(k * plen, plen)
        return pltpu.make_async_copy(ph_ref.at[at], ph.at[at], sem_h.at[2 + k])

    load_w = pltpu.make_async_copy(proj_ref, proj, sem_h.at[2 + n_p])
    load_w.start()
    for k in range(2):
        load_q(k).start()

    barrier = pltpu.get_barrier_semaphore()
    pl.semaphore_signal(barrier, inc=1, device_id=partner, device_id_type=MESH)

    for k in range(1, n_pa):
        pl.semaphore_signal(barrier, inc=1, device_id=plane(k), device_id_type=MESH)
    for k in range(1, n_z):
        pl.semaphore_signal(barrier, inc=1, device_id=line_z(k), device_id_type=MESH)

    for k in range(n_p):
        load_p(k).start()

    lane = lax.broadcasted_iota(jnp.int32, (queries, 128), 1)
    line = lax.broadcasted_iota(jnp.int32, (queries, 128), 0)
    place = (lane == line + (me % 8) * queries).astype(F32)
    cbuf[me] = jnp.concatenate([dot(cand_ref[...].astype(F32), place, 0, 0), jnp.zeros((16 - cand_count, 128), F32)], axis=0).astype(BF16)
    score[...] = jnp.zeros_like(score)
    acc[...] = jnp.zeros_like(acc)

    def shift(h, d1, d2):
        dx, dy = (d1, d2) if h == 0 else (d2, d1)
        return dy % SIDE * SIDE + dx % SIDE

    def slot(h, d1, d2):
        return at_offset[shift(h, d1, d2)]

    def neighbour(h, g, o):
        return plane(shift(h, o, 0) if g == 0 else shift(h, 0, o))

    def piece_of(h, g, o, k, to, first, count):
        d1, d2 = (o, 0) if g == 0 else (g - 1, o)
        block = gq.at[slot(h, d1, d2), pl.ds(h * hrow + first, count)]
        return remote(block, block, a_s, a_r.at[(h * 5 + g) * 4 + k], neighbour(h, g, to))

    def whole(h, g, o, k, to):
        return piece_of(h, g, o, k, to, 0, hrow)

    def quarter(h, g, o, k, to):
        return piece_of(h, g, o, k, to, (k - 2) * qrow, qrow)

    def send_whole(h, g):
        whole(h, g, 0, 0, 1).start()
        whole(h, g, 0, 1, 3).start()

    def pass_on(h, g):
        whole(h, g, 3, 0, 1).wait_recv()
        quarter(h, g, 3, 2, 1).start()
        whole(h, g, 1, 1, 3).wait_recv()
        quarter(h, g, 1, 3, 3).start()

    def finish(h, g):
        quarter(h, g, 2, 2, 1).wait_recv()
        quarter(h, g, 2, 3, 3).wait_recv()

    def to_all(buf, send, recv):
        for k in FAR:
            remote(buf.at[me], buf.at[me], send, recv, plane(k)).start()

    def many(buf, count, send, recv):
        part_of = buf.at[pl.ds(0, count)]
        return remote(part_of, part_of, send, recv, partner)

    for h in range(2):
        at = pl.ds(h * hrow, hrow)
        if h == 0:
            load_w.wait()
        load_q(h).wait()
        e = dot(qh[at, :], proj[...])
        qe[at, :] = e
        gq[me, at, :] = (e * inverse_norm(e)).astype(BF16)
        if h == 0:
            pl.semaphore_wait(barrier, n_pa + n_z - 1)
        send_whole(h, 0)
        send_whole(h, 1)

    to_all(cbuf, c_s, c_r)

    def project_passage(k):
        load_p(k).wait()
        at = pl.ds(k * plen, plen)
        e = dot(ph[at, :], proj[...])
        pe[at, :] = e
        u = (e * inverse_norm(e)).astype(BF16)
        pone[k, :, 0:vec] = u
        pone[k, :, vec:] = jnp.ones((plen, vec), BF16)
        pt[k] = u.astype(F32).T.astype(BF16)

    project_passage(0)

    for h in range(2):
        pass_on(h, 0)
        send_whole(h, 2)
        send_whole(h, 4)

    project_passage(1)

    for h in range(2):
        pass_on(h, 1)

    for k in range(2, n_p):
        project_passage(k)

    narrow = lax.broadcasted_iota(jnp.int32, (8, 128), 1)

    @pl.loop(0, n_pa)
    def _(k):
        @pl.when(k == 2)
        def _():
            for h in range(2):
                finish(h, 0)
                send_whole(h, 3)

        @pl.when(k == 4)
        def _():
            for h in range(2):
                pass_on(h, 2)
                pass_on(h, 4)

        @pl.when(k == 7)
        def _():
            for h in range(2):
                pass_on(h, 3)

        @pl.when(k == 9)
        def _():
            for h in range(2):
                finish(h, 1)

        @pl.when(k == 11)
        def _():
            for h in range(2):
                finish(h, 2)
                finish(h, 4)

        @pl.when(k == 15)
        def _():
            for h in range(2):
                finish(h, 3)

        b = pick(k, [at_offset[dy * SIDE + dx] for dx, dy in ORDER])
        u = gq[b]
        at = pl.ds(pl.multiple_of(b * rows_q, rows_q), rows_q)
        for p in range(n_p):
            e = jnp.exp2(dot(u, pt[p]) * (LOG2E * scale)).astype(BF16)
            ex[p, at, :] = e
            sums = dot(e, pone[p])
            total = sums[:, vec:]
            inverse = 1.0 / total
            gn[p, at, :] = (sums[:, :vec] * inverse).astype(BF16)
            qn[p, at, :] = (u.astype(F32) * inverse).astype(BF16)
            four = total.reshape(queries, 4, qlen // 4, vec)
            logs = jnp.log((four[:, 0] * four[:, 1]) * (four[:, 2] * four[:, 3]))
            s = acc[p, b // 8]
            for i in range(queries):
                s = s + jnp.where(narrow == lax.rem(b, 8) * queries + i, logs[i], 0.0)
            acc[p, b // 8] = s

    for p in range(n_p):
        for i in range(2):
            score[me, p:p + 1, i * 128:(i + 1) * 128] = sharpness_divisor * jnp.sum(acc[p, i], axis=0, keepdims=True)

    to_all(score, sc_s, sc_r)
    many(cbuf, n_pa - 1, c_s, c_r).wait_recv()

    left, right = cbuf[0].astype(F32), cbuf[8].astype(F32)
    for i in range(1, 8):
        left = left + cbuf[i].astype(F32)
        right = right + cbuf[8 + i].astype(F32)
    named = jnp.concatenate([left, right], axis=1).astype(jnp.int32)
    rank = lax.broadcasted_iota(jnp.int32, (8, 256), 0)

    @pl.loop(0, n_pa)
    def _(o):
        ident = jnp.where(rank < n_p, o * n_p + rank, -1)
        first = (named[0:1, :] == ident).astype(F32)
        found = first
        for c in range(1, cand_count):
            found = found + (named[c:c + 1, :] == ident).astype(F32)
        mask[o] = found
        mark[o] = first

    many(score, n_pa - 1, sc_s, sc_r).wait_recv()

    similarity = score[...]
    exponent = jnp.exp(similarity) * mask[...]
    element_total = jnp.sum(jnp.sum(exponent, axis=0), axis=0, keepdims=True)
    chosen = jnp.sum(jnp.sum(similarity * mark[...], axis=0), axis=0, keepdims=True)
    loss = jnp.log(element_total) - chosen
    mine_row = lax.broadcasted_iota(jnp.int32, (queries, 256), 1) == lax.broadcasted_iota(
        jnp.int32, (queries, 256), 0) + me * queries
    column = jnp.sum(jnp.where(mine_row, loss, 0.0), axis=1, keepdims=True)
    loss_ref[...] = jnp.sum(jnp.where(lane == line, column, 0.0), axis=0, keepdims=True)
    grad_score = (jnp.exp(score[me]) * mask[me] / element_total - mark[me]) * (1.0 / vec)
    for p in range(n_p):
        gsrep[p] = jnp.broadcast_to(grad_score[p:p + 1, :], (vec, 256)).T

    q_half = queries // 2

    def spread(p, b, h, count):
        g = gsrep[p, pl.ds(pl.multiple_of(b * queries + h * q_half, 8), count), :]
        return jnp.broadcast_to(g[:, None, :], (count, qlen, vec)).reshape(count * qlen, vec)

    def value(h, g, o):
        if g == 0:
            return sum1[h * SIDE + o]
        b = slot(h, g - 1, o)
        at = pl.ds(pl.multiple_of(b * rows_q + h * hrow, hrow), hrow)
        result = spread(0, b, h, q_half) * gn[0, at, :].astype(F32)
        for p in range(1, n_p):
            result = result + spread(p, b, h, q_half) * gn[p, at, :].astype(F32)
        return result

    def leg1(h, g, k, to):
        i = h * 5 + g
        at = pl.ds(k * qrow, qrow)
        return remote(sbuf1.at[i, at], rbuf1.at[i, at], b_s, b_r.at[i * 4 + k], neighbour(h, g, to))

    def leg2(h, g, k, to):
        i = h * 5 + g
        return remote(sbuf2.at[i * 2 + k], rbuf2.at[i * 2 + k], b_s, b_r.at[i * 4 + 2 + k],
                      neighbour(h, g, to))

    def step1(h, g):
        sbuf1[h * 5 + g] = value(h, g, 2).astype(BF16)
        leg1(h, g, 0, 1).start()
        leg1(h, g, 1, 3).start()

    def step2(h, g):
        i = h * 5 + g
        v = value(h, g, 1)
        leg1(h, g, 0, 1).wait_recv()
        sbuf2[i * 2, 0:qrow, :] = (v[0:qrow] + rbuf1[i, 0:qrow, :].astype(F32)).astype(BF16)
        sbuf2[i * 2, qrow:, :] = v[qrow:].astype(BF16)
        leg2(h, g, 0, 1).start()
        v = value(h, g, 3)
        leg1(h, g, 1, 3).wait_recv()
        sbuf2[i * 2 + 1, 0:qrow, :] = v[0:qrow].astype(BF16)
        sbuf2[i * 2 + 1, qrow:, :] = (v[qrow:] + rbuf1[i, qrow:, :].astype(F32)).astype(BF16)
        leg2(h, g, 1, 3).start()

    def step3(h, g):
        i = h * 5 + g
        v = value(h, g, 0)
        leg2(h, g, 0, 1).wait_recv()
        v = v + rbuf2[i * 2].astype(F32)
        leg2(h, g, 1, 3).wait_recv()
        return v + rbuf2[i * 2 + 1].astype(F32)

    def grad_passage(first, last):
        @pl.loop(first, last)
        def _(b):
            at = pl.ds(pl.multiple_of(b * rows_q, rows_q), rows_q)
            for p in range(n_p):
                w = (spread(p, b, 0, queries) * qn[p, at, :].astype(F32)).astype(BF16)
                gp[p] += dot(ex[p, at, :], w, 0, 0)

    gp[...] = jnp.zeros_like(gp)

    for i in range(8):
        step1(i % 2, 1 + (i // 2 + 2) % SIDE)

    grad_passage(0, 5)

    for i in range(8):
        step2(i % 2, 1 + (i // 2 + 2) % SIDE)

    grad_passage(5, 16)

    for h in range(2):
        sum1[h * SIDE + 2] = step3(h, 3)
        step1(h, 0)

    for p in range(n_p):
        at = pl.ds(p * plen, plen)
        g = norm_backward(pe[at, :], gp[p])
        pg_ref[at, :] = g
        pgb[at, :] = g.astype(BF16)

    quarter_rows = width // 8

    def passage_product(first, last):
        @pl.loop(first, last)
        def _(c):
            at = pl.ds(pl.multiple_of(c * quarter_rows, quarter_rows), quarter_rows)
            wg[at, :] = dot(ph[:, at], pgb[...], 0, 0)

    passage_product(0, 3)

    for h in range(2):
        sum1[h * SIDE + 1] = step3(h, 2)
        sum1[h * SIDE + 3] = step3(h, 4)
        step2(h, 0)
        sum1[h * SIDE] = step3(h, 1)

    passage_product(3, 8)

    for h in range(2):
        at = pl.ds(h * hrow, hrow)
        g = norm_backward(qe[at, :], step3(h, 0))
        qg_ref[at, :] = g
        qgb[at, :] = g.astype(BF16)

    half_rows = width // 2
    chunk = half_rows // n_pa
    base = core * half_rows

    def swap(j):
        at = pl.ds(pl.multiple_of(lax.rem(y + 1 + j, SIDE) * quarter_rows, quarter_rows), quarter_rows)
        return remote(half.at[at], got0.at[at], s0, r0.at[j], partner)

    def product(first, j):
        at = pl.ds(pl.multiple_of(first + lax.rem(y + 1 + j, SIDE) * quarter_rows, quarter_rows), quarter_rows)
        return wg[at, :] + dot(qh[:, at], qgb[...], 0, 0)

    @pl.loop(0, SIDE)
    def _(j):
        at = pl.ds(pl.multiple_of(lax.rem(y + 1 + j, SIDE) * quarter_rows, quarter_rows), quarter_rows)
        half[at, :] = product(half_rows - base, j).astype(BF16)
        swap(j).start()

    def to_xy(peer):
        return remote(part.at[peer], got1.at[me], s1, r1, {"pa": peer})

    @pl.loop(0, SIDE)
    def _(j):
        v = product(base, j)
        row = lax.rem(y + 1 + j, SIDE)
        swap(j).wait_recv()
        v = v + got0[pl.ds(pl.multiple_of(row * quarter_rows, quarter_rows), quarter_rows), :].astype(F32)
        for i in range(SIDE):
            part[row * SIDE + i] = v[i * chunk:(i + 1) * chunk].astype(BF16)

            @pl.when((row == y) & (x == i))
            def _():
                mine[...] = v[i * chunk:(i + 1) * chunk]

        for i in range(1, SIDE):
            to_xy(row * SIDE + columns[i]).start()

        @pl.when(j < SIDE - 1)
        def _():
            to_xy(row * SIDE + x).start()

    many(got1, n_pa - 1, s1, r1).wait_recv()
    total = mine[...]
    for k in range(1, n_pa):
        total = total + got1[at_offset[k]].astype(F32)
    total = total.astype(BF16)
    part[me] = total
    got2[z] = total
    for k in range(1, n_z):
        remote(part.at[me], got2.at[z], s2, r2, line_z(k)).start()
    if n_z > 1:
        many(got2, n_z - 1, s2, r2).wait_recv()
    total = got2[0].astype(F32)
    for k in range(1, n_z):
        total = total + got2[k].astype(F32)
    out[pl.ds(base + me * chunk, chunk), :] = total.astype(BF16)

    def chunk_at(first, who):
        return out.at[pl.ds(first + who * chunk, chunk)]

    def back_xy(k, who, recv):
        return remote(chunk_at(base, who), chunk_at(base, who), s4, r4.at[recv], plane(k))

    def across(k):
        here = chunk_at(base, at_offset[k])
        return remote(here, here, s5, r5, partner)

    for k in FAR:
        back_xy(k, me, back(k)).start()
    across(0).start()
    for k in FAR[::-1]:
        back_xy(k, at_offset[k], k).wait_recv()
        across(k).start()
    many(out, half_rows, s5, r5).wait_recv()
    wg_ref[...] = out[...]

    many(gq, n_pa - 1, a_s, a_s).wait_send()
    many(sbuf1, 10, b_s, b_s).wait_send()
    many(sbuf2, 20, b_s, b_s).wait_send()
    many(cbuf, n_pa - 1, c_s, c_r).wait_send()
    many(score, n_pa - 1, sc_s, sc_r).wait_send()
    many(half, half_rows, s0, s0).wait_send()
    many(part, n_pa - 1, s1, r1).wait_send()
    if n_z > 1:
        many(got2, n_z - 1, s2, r2).wait_send()
    many(out, chunk * (n_pa - 1), s4, s4).wait_send()
    many(out, half_rows, s5, r5).wait_send()


def hand_over(loss_ref, qg_ref, pg_ref, wg_ref, loss_out, qg_out, pg_out, wg_out):
    loss_out[...] = loss_ref[:, 0:loss_out.shape[1]]
    qg_out[...] = qg_ref[...]
    pg_out[...] = pg_ref[...]
    wg_out[...] = wg_ref[...].astype(F32)


def shards(query_hidden, passage_hidden, projection, candidates):
    queries, qlen, width = query_hidden.shape
    n_p, plen, _ = passage_hidden.shape
    vec = projection.shape[1]
    n_pa, n_z = lax.axis_size("pa"), lax.axis_size("pb") // 2
    rows_q, rows_p = queries * qlen, n_p * plen
    all_rows = n_pa * rows_q
    hrow = rows_q // 2
    half_rows = width // 2
    chunk = half_rows // n_pa
    dma = pltpu.SemaphoreType.DMA
    V = pltpu.VMEM
    in_vmem, anywhere = pl.BlockSpec(memory_space=pltpu.VMEM), pl.BlockSpec(memory_space=pl.ANY)
    loss, query_grad, passage_grad, weight_grad = pl.pallas_call(
        functools.partial(kernel, n_z, qlen, candidates.shape[1]),
        out_shape=(
            jax.ShapeDtypeStruct((1, 128), F32),
            jax.ShapeDtypeStruct((rows_q, vec), F32),
            jax.ShapeDtypeStruct((rows_p, vec), F32),
            jax.ShapeDtypeStruct((width, vec), BF16),
        ),
        in_specs=[anywhere, anywhere, anywhere, in_vmem],
        out_specs=(in_vmem,) * 4,
        scratch_shapes=[
            V((width, vec), BF16), V((rows_q, width), BF16), V((rows_p, width), BF16), V((rows_q, vec), F32), V((rows_p, vec), F32),
            V((n_p, vec, plen), BF16), V((n_p, plen, 2 * vec), BF16), V((n_pa, rows_q, vec), BF16),
            V((n_p, all_rows, plen), BF16), V((n_p, all_rows, vec), BF16), V((n_p, all_rows, vec), BF16),
            V((n_p, 2, 8, 128), F32), V((n_pa, 16, 128), BF16), V((n_pa, 8, 256), F32), V((n_pa, 8, 256), F32),
            V((n_pa, 8, 256), F32), V((n_p, 256, vec), F32),
            V((10, hrow, vec), BF16), V((20, hrow, vec), BF16), V((10, hrow, vec), BF16), V((20, hrow, vec), BF16),
            V((2 * SIDE, hrow, vec), F32), V((n_p, plen, vec), F32), V((rows_q, vec), BF16), V((rows_p, vec), BF16),
            V((width, vec), F32), V((width, vec), BF16), V((half_rows, vec), BF16), V((half_rows, vec), BF16),
            V((n_pa, chunk, vec), BF16), V((n_pa, chunk, vec), BF16), V((chunk, vec), F32), V((n_z, chunk, vec), BF16),
            dma((3 + n_p,)), dma, dma, dma, dma, dma, dma((40,)), dma, dma((40,)),
            dma, dma((SIDE,)), dma, dma, dma, dma, dma, dma((n_pa,)), dma, dma,
        ],
        compiler_params=pltpu.CompilerParams(collective_id=0, has_side_effects=True, vmem_limit_bytes=60 * 2**20),
        name="retriever",
    )(query_hidden.reshape(rows_q, width), passage_hidden.reshape(rows_p, width), projection, candidates)
    loss, query_grad, passage_grad, weight_grad = pl.pallas_call(
        hand_over,
        out_shape=(
            jax.ShapeDtypeStruct((1, queries), F32),
            jax.ShapeDtypeStruct((rows_q, vec), F32),
            jax.ShapeDtypeStruct((rows_p, vec), F32),
            jax.ShapeDtypeStruct((width, vec), F32),
        ),
        in_specs=[in_vmem] * 4,
        out_specs=(in_vmem,) * 4,
        name="hand_over",
    )(loss, query_grad, passage_grad, weight_grad)
    return (
        loss.reshape(queries),
        query_grad.reshape(queries, qlen, vec),
        passage_grad.reshape(n_p, plen, vec),
        weight_grad,
    )


def solution(mesh):
    placed = (P(("pb", "pa"), None, None), P(("pb", "pa"), None, None), P(), P(("pb", "pa"), None))
    return jax.shard_map(
        shards,
        mesh=mesh,
        in_specs=placed,
        out_specs=(P(("pb", "pa")), P(("pb", "pa"), None, None), P(("pb", "pa"), None, None), P()),
        check_vma=False,
    )
```

```python
import functools
import jax
import jax.numpy as jnp
from jax import lax
from jax.experimental import pallas as pl
from jax.experimental.pallas import tpu as pltpu
from jax.sharding import PartitionSpec as P

MESH = pl.DeviceIdType.MESH
F32, BF16 = jnp.float32, jnp.bfloat16
SIDE = 4
sharpness_divisor = 0.1
epsilon = 1e-06
LOG2E = 1.4426950408889634


def remote(src, dst, send, recv, device):
    return pltpu.make_async_remote_copy(
        src_ref=src, dst_ref=dst, send_sem=send, recv_sem=recv, device_id=device, device_id_type=MESH
    )


def dot(a, b, ca=1, cb=0):
    return lax.dot_general(a, b, (((ca,), (cb,)), ((), ())), preferred_element_type=F32)


def inverse_norm(embedded):
    return lax.rsqrt(jnp.mean(embedded * embedded, axis=-1, keepdims=True) + epsilon)


def norm_backward(embedded, unit_grad):
    inv_norm = inverse_norm(embedded)
    inner_mean = jnp.mean(embedded * unit_grad, axis=-1, keepdims=True)
    return inv_norm * unit_grad - inv_norm * inv_norm * inv_norm * embedded * inner_mean


def pick(k, values):
    result = values[0]
    for i, v in enumerate(values[1:]):
        result = jnp.where(k == i + 1, v, result)
    return result


FAR = [10, 9, 11, 6, 14, 2, 8, 5, 7, 13, 15, 1, 3, 4, 12]
ORDER = [(0, 0), (1, 0), (3, 0), (0, 1), (0, 3), (1, 1), (1, 3), (3, 1), (3, 3),
         (2, 0), (0, 2), (2, 1), (2, 3), (1, 2), (3, 2), (2, 2)]


def kernel(n_z, qlen, cand_count,
           qh_ref, ph_ref, proj_ref, cand_ref,
           loss_ref, qg_ref, pg_ref, wg_ref,
           proj, qh, ph, qe, pe, pt, pone, gq, ex, gn, qn, acc, cbuf, mask, mark, score, gsrep,
           sbuf1, sbuf2, rbuf1, rbuf2, sum1, gp, qgb, pgb,
           wg, out, half, got0, part, got1, mine, got2,
           sem_h, c_s, c_r, sc_s, sc_r, a_s, a_r, b_s, b_r,
           s0, r0, s1, r1, s2, r2, s4, r4, s5, r5):
    n_pa = SIDE * SIDE
    rows_q = qh.shape[0]
    hrow = rows_q // 2
    qrow = hrow // 2
    queries = rows_q // qlen
    n_p, plen = pone.shape[0], pone.shape[1]
    width = qh.shape[1]
    vec = proj.shape[1]
    me, pb = lax.axis_index("pa"), lax.axis_index("pb")
    y, x = me // SIDE, me % SIDE
    z, core = pb // 2, pb % 2
    partner = {"pb": z * 2 + (1 - core)}
    scale = 1.0 / (vec * sharpness_divisor)

    rows = [lax.rem(y + d, SIDE) * SIDE for d in range(SIDE)]
    columns = [lax.rem(x + d, SIDE) for d in range(SIDE)]
    at_offset = [rows[k // SIDE] + columns[k % SIDE] for k in range(n_pa)]
    along_z = [lax.rem(z + k, n_z) for k in range(n_z)]

    def back(k):
        return (SIDE - k // SIDE) % SIDE * SIDE + (SIDE - k % SIDE) % SIDE

    def plane(k):
        return {"pa": at_offset[k]}

    def line_z(k):
        return {"pb": along_z[k] * 2 + core}

    def load_q(k):
        at = pl.ds(k * hrow, hrow)
        return pltpu.make_async_copy(qh_ref.at[at], qh.at[at], sem_h.at[k])

    def load_p(k):
        at = pl.ds(k * plen, plen)
        return pltpu.make_async_copy(ph_ref.at[at], ph.at[at], sem_h.at[2 + k])

    load_w = pltpu.make_async_copy(proj_ref, proj, sem_h.at[2 + n_p])
    load_w.start()
    for k in range(2):
        load_q(k).start()

    barrier = pltpu.get_barrier_semaphore()
    pl.semaphore_signal(barrier, inc=1, device_id=partner, device_id_type=MESH)

    for k in range(1, n_pa):
        pl.semaphore_signal(barrier, inc=1, device_id=plane(k), device_id_type=MESH)
    for k in range(1, n_z):
        pl.semaphore_signal(barrier, inc=1, device_id=line_z(k), device_id_type=MESH)

    for k in range(n_p):
        load_p(k).start()

    lane = lax.broadcasted_iota(jnp.int32, (queries, 128), 1)
    line = lax.broadcasted_iota(jnp.int32, (queries, 128), 0)
    place = (lane == line + (me % 8) * queries).astype(F32)
    cbuf[me] = jnp.concatenate([dot(cand_ref[...].astype(F32), place, 0, 0), jnp.zeros((16 - cand_count, 128), F32)], axis=0).astype(BF16)
    score[...] = jnp.zeros_like(score)
    acc[...] = jnp.zeros_like(acc)

    def shift(h, d1, d2):
        dx, dy = (d1, d2) if h == 0 else (d2, d1)
        return dy % SIDE * SIDE + dx % SIDE

    def slot(h, d1, d2):
        return at_offset[shift(h, d1, d2)]

    def neighbour(h, g, o):
        return plane(shift(h, o, 0) if g == 0 else shift(h, 0, o))

    def piece_of(h, g, o, k, to, first, count):
        d1, d2 = (o, 0) if g == 0 else (g - 1, o)
        block = gq.at[slot(h, d1, d2), pl.ds(h * hrow + first, count)]
        return remote(block, block, a_s, a_r.at[(h * 5 + g) * 4 + k], neighbour(h, g, to))

    def whole(h, g, o, k, to):
        return piece_of(h, g, o, k, to, 0, hrow)

    def quarter(h, g, o, k, to):
        return piece_of(h, g, o, k, to, (k - 2) * qrow, qrow)

    def send_whole(h, g):
        whole(h, g, 0, 0, 1).start()
        whole(h, g, 0, 1, 3).start()

    def pass_on(h, g):
        whole(h, g, 3, 0, 1).wait_recv()
        quarter(h, g, 3, 2, 1).start()
        whole(h, g, 1, 1, 3).wait_recv()
        quarter(h, g, 1, 3, 3).start()

    def finish(h, g):
        quarter(h, g, 2, 2, 1).wait_recv()
        quarter(h, g, 2, 3, 3).wait_recv()

    def to_all(buf, send, recv):
        for k in FAR:
            remote(buf, buf, send, recv, plane(k)).start()

    def scores_in():
        part_of = score.at[pl.ds(0, n_pa - 1), pl.ds(0, 4)]
        return remote(part_of, part_of, sc_s, sc_r, partner)

    def many(buf, count, send, recv):
        part_of = buf.at[pl.ds(0, count)]
        return remote(part_of, part_of, send, recv, partner)

    for h in range(2):
        at = pl.ds(h * hrow, hrow)
        if h == 0:
            load_w.wait()
        load_q(h).wait()
        e = dot(qh[at, :], proj[...])
        qe[at, :] = e
        gq[me, at, :] = (e * inverse_norm(e)).astype(BF16)
        if h == 0:
            pl.semaphore_wait(barrier, n_pa + n_z - 1)
        send_whole(h, 0)
        send_whole(h, 1)

    to_all(cbuf.at[me], c_s, c_r)

    def project_passage(k):
        load_p(k).wait()
        at = pl.ds(k * plen, plen)
        e = dot(ph[at, :], proj[...])
        pe[at, :] = e
        u = (e * inverse_norm(e)).astype(BF16)
        pone[k, :, 0:vec] = u
        pone[k, :, vec:] = jnp.ones((plen, vec), BF16)
        pt[k] = u.astype(F32).T.astype(BF16)

    project_passage(0)

    for h in range(2):
        pass_on(h, 0)
        send_whole(h, 2)
        send_whole(h, 4)

    project_passage(1)

    for h in range(2):
        pass_on(h, 1)

    for k in range(2, n_p):
        project_passage(k)

    narrow = lax.broadcasted_iota(jnp.int32, (8, 128), 1)

    @pl.loop(0, n_pa)
    def _(k):
        @pl.when(k == 3)
        def _():
            for h in range(2):
                finish(h, 0)
                send_whole(h, 3)

        @pl.when(k == 5)
        def _():
            for h in range(2):
                pass_on(h, 2)
                pass_on(h, 4)

        @pl.when(k == 9)
        def _():
            for h in range(2):
                pass_on(h, 3)

        @pl.when(k == 9)
        def _():
            for h in range(2):
                finish(h, 1)

        @pl.when(k == 11)
        def _():
            for h in range(2):
                finish(h, 2)
                finish(h, 4)

        @pl.when(k == 15)
        def _():
            for h in range(2):
                finish(h, 3)

        b = pick(k, [at_offset[dy * SIDE + dx] for dx, dy in ORDER])
        u = gq[b]
        at = pl.ds(pl.multiple_of(b * rows_q, rows_q), rows_q)
        for p in range(n_p):
            e = jnp.exp2(dot(u, pt[p]) * (LOG2E * scale)).astype(BF16)
            ex[p, at, :] = e
            sums = dot(e, pone[p])
            total = sums[:, vec:]
            inverse = 1.0 / total
            gn[p, at, :] = (sums[:, :vec] * inverse).astype(BF16)
            qn[p, at, :] = (u.astype(F32) * inverse).astype(BF16)
            four = total.reshape(queries, 4, qlen // 4, vec)
            logs = jnp.log((four[:, 0] * four[:, 1]) * (four[:, 2] * four[:, 3]))
            s = acc[p, b // 8]
            for i in range(queries):
                s = s + jnp.where(narrow == lax.rem(b, 8) * queries + i, logs[i], 0.0)
            acc[p, b // 8] = s

    for p in range(n_p):
        for i in range(2):
            score[me, p:p + 1, i * 128:(i + 1) * 128] = sharpness_divisor * jnp.sum(acc[p, i], axis=0, keepdims=True)

    to_all(score.at[me, pl.ds(0, 4)], sc_s, sc_r)
    many(cbuf, n_pa - 1, c_s, c_r).wait_recv()

    left, right = cbuf[0].astype(F32), cbuf[8].astype(F32)
    for i in range(1, 8):
        left = left + cbuf[i].astype(F32)
        right = right + cbuf[8 + i].astype(F32)
    named = jnp.concatenate([left, right], axis=1).astype(jnp.int32)
    rank = lax.broadcasted_iota(jnp.int32, (8, 256), 0)

    @pl.loop(0, n_pa)
    def _(o):
        ident = jnp.where(rank < n_p, o * n_p + rank, -1)
        first = (named[0:1, :] == ident).astype(F32)
        found = first
        for c in range(1, cand_count):
            found = found + (named[c:c + 1, :] == ident).astype(F32)
        mask[o] = found
        mark[o] = first

    scores_in().wait_recv()

    similarity = score[...]
    exponent = jnp.exp(similarity) * mask[...]
    element_total = jnp.sum(jnp.sum(exponent, axis=0), axis=0, keepdims=True)
    chosen = jnp.sum(jnp.sum(similarity * mark[...], axis=0), axis=0, keepdims=True)
    loss = jnp.log(element_total) - chosen
    mine_row = lax.broadcasted_iota(jnp.int32, (queries, 256), 1) == lax.broadcasted_iota(
        jnp.int32, (queries, 256), 0) + me * queries
    column = jnp.sum(jnp.where(mine_row, loss, 0.0), axis=1, keepdims=True)
    loss_ref[...] = jnp.sum(jnp.where(lane == line, column, 0.0), axis=0, keepdims=True)
    grad_score = (jnp.exp(score[me]) * mask[me] / element_total - mark[me]) * (1.0 / vec)
    for p in range(n_p):
        gsrep[p] = jnp.broadcast_to(grad_score[p:p + 1, :], (vec, 256)).T

    q_half = queries // 2

    def spread(p, b, h, count):
        g = gsrep[p, pl.ds(pl.multiple_of(b * queries + h * q_half, 8), count), :]
        return jnp.broadcast_to(g[:, None, :], (count, qlen, vec)).reshape(count * qlen, vec)

    def value(h, g, o):
        if g == 0:
            return sum1[h * SIDE + o]
        b = slot(h, g - 1, o)
        at = pl.ds(pl.multiple_of(b * rows_q + h * hrow, hrow), hrow)
        result = spread(0, b, h, q_half) * gn[0, at, :].astype(F32)
        for p in range(1, n_p):
            result = result + spread(p, b, h, q_half) * gn[p, at, :].astype(F32)
        return result

    def leg1(h, g, k, to):
        i = h * 5 + g
        at = pl.ds(k * qrow, qrow)
        return remote(sbuf1.at[i, at], rbuf1.at[i, at], b_s, b_r.at[i * 4 + k], neighbour(h, g, to))

    def leg2(h, g, k, to):
        i = h * 5 + g
        return remote(sbuf2.at[i * 2 + k], rbuf2.at[i * 2 + k], b_s, b_r.at[i * 4 + 2 + k],
                      neighbour(h, g, to))

    def step1(h, g):
        sbuf1[h * 5 + g] = value(h, g, 2).astype(BF16)
        leg1(h, g, 0, 1).start()
        leg1(h, g, 1, 3).start()

    def step2(h, g):
        i = h * 5 + g
        v = value(h, g, 1)
        leg1(h, g, 0, 1).wait_recv()
        sbuf2[i * 2, 0:qrow, :] = (v[0:qrow] + rbuf1[i, 0:qrow, :].astype(F32)).astype(BF16)
        sbuf2[i * 2, qrow:, :] = v[qrow:].astype(BF16)
        leg2(h, g, 0, 1).start()
        v = value(h, g, 3)
        leg1(h, g, 1, 3).wait_recv()
        sbuf2[i * 2 + 1, 0:qrow, :] = v[0:qrow].astype(BF16)
        sbuf2[i * 2 + 1, qrow:, :] = (v[qrow:] + rbuf1[i, qrow:, :].astype(F32)).astype(BF16)
        leg2(h, g, 1, 3).start()

    def step3(h, g):
        i = h * 5 + g
        v = value(h, g, 0)
        leg2(h, g, 0, 1).wait_recv()
        v = v + rbuf2[i * 2].astype(F32)
        leg2(h, g, 1, 3).wait_recv()
        return v + rbuf2[i * 2 + 1].astype(F32)

    def grad_passage(first, last):
        @pl.loop(first, last)
        def _(b):
            at = pl.ds(pl.multiple_of(b * rows_q, rows_q), rows_q)
            for p in range(n_p):
                w = (spread(p, b, 0, queries) * qn[p, at, :].astype(F32)).astype(BF16)
                gp[p] += dot(w.T, ex[p, at, :])

    gp[...] = jnp.zeros_like(gp)

    for i in range(8):
        step1(i % 2, 1 + (i // 2 + 2) % SIDE)

    grad_passage(0, 5)

    for i in range(8):
        step2(i % 2, 1 + (i // 2 + 2) % SIDE)

    grad_passage(5, 16)

    for h in range(2):
        sum1[h * SIDE + 2] = step3(h, 3)
        step1(h, 0)

    for p in range(n_p):
        at = pl.ds(p * plen, plen)
        g = norm_backward(pe[at, :], gp[p].T)
        pg_ref[at, :] = g
        pgb[:, at] = g.T.astype(BF16)

    quarter_rows = width // 8

    def passage_product(first, last):
        @pl.loop(first, last)
        def _(c):
            at = pl.ds(pl.multiple_of(c * quarter_rows, quarter_rows), quarter_rows)
            wg[at, :] = dot(pgb[...], ph[:, at]).T

    passage_product(0, 3)

    for h in range(2):
        sum1[h * SIDE + 1] = step3(h, 2)
        sum1[h * SIDE + 3] = step3(h, 4)
        step2(h, 0)
        sum1[h * SIDE] = step3(h, 1)

    passage_product(3, 8)

    for h in range(2):
        at = pl.ds(h * hrow, hrow)
        g = norm_backward(qe[at, :], step3(h, 0))
        qg_ref[at, :] = g
        qgb[:, at] = g.T.astype(BF16)

    half_rows = width // 2
    chunk = half_rows // n_pa
    base = core * half_rows

    def swap(j):
        at = pl.ds(pl.multiple_of(lax.rem(y + 1 + j, SIDE) * quarter_rows, quarter_rows), quarter_rows)
        return remote(half.at[at], got0.at[at], s0, r0.at[j], partner)

    def product(first, j):
        at = pl.ds(pl.multiple_of(first + lax.rem(y + 1 + j, SIDE) * quarter_rows, quarter_rows), quarter_rows)
        return wg[at, :] + dot(qgb[...], qh[:, at]).T

    @pl.loop(0, SIDE)
    def _(j):
        at = pl.ds(pl.multiple_of(lax.rem(y + 1 + j, SIDE) * quarter_rows, quarter_rows), quarter_rows)
        half[at, :] = product(half_rows - base, j).astype(BF16)
        swap(j).start()

    def to_xy(peer):
        return remote(part.at[peer], got1.at[me], s1, r1, {"pa": peer})

    @pl.loop(0, SIDE)
    def _(j):
        v = product(base, j)
        row = lax.rem(y + 1 + j, SIDE)
        swap(j).wait_recv()
        v = v + got0[pl.ds(pl.multiple_of(row * quarter_rows, quarter_rows), quarter_rows), :].astype(F32)
        for i in range(SIDE):
            part[row * SIDE + i] = v[i * chunk:(i + 1) * chunk].astype(BF16)

            @pl.when((row == y) & (x == i))
            def _():
                mine[...] = v[i * chunk:(i + 1) * chunk]

        for i in range(1, SIDE):
            to_xy(row * SIDE + columns[i]).start()

        @pl.when(j < SIDE - 1)
        def _():
            to_xy(row * SIDE + x).start()

    many(got1, n_pa - 1, s1, r1).wait_recv()
    total = mine[...]
    for k in range(1, n_pa):
        total = total + got1[at_offset[k]].astype(F32)
    total = total.astype(BF16)
    part[me] = total
    got2[z] = total
    for k in range(1, n_z):
        remote(part.at[me], got2.at[z], s2, r2, line_z(k)).start()
    if n_z > 1:
        many(got2, n_z - 1, s2, r2).wait_recv()
    total = got2[0].astype(F32)
    for k in range(1, n_z):
        total = total + got2[k].astype(F32)
    out[pl.ds(base + me * chunk, chunk), :] = total.astype(BF16)

    def chunk_at(first, who):
        return out.at[pl.ds(first + who * chunk, chunk)]

    def back_xy(k, who, recv):
        return remote(chunk_at(base, who), chunk_at(base, who), s4, r4.at[recv], plane(k))

    def across(k):
        here = chunk_at(base, at_offset[k])
        return remote(here, here, s5, r5, partner)

    for k in FAR:
        back_xy(k, me, back(k)).start()
    across(0).start()
    for k in FAR[::-1]:
        back_xy(k, at_offset[k], k).wait_recv()
        across(k).start()
    many(out, half_rows, s5, r5).wait_recv()
    wg_ref[...] = out[...]

    many(gq, n_pa - 1, a_s, a_s).wait_send()
    many(sbuf1, 10, b_s, b_s).wait_send()
    many(sbuf2, 20, b_s, b_s).wait_send()
    many(cbuf, n_pa - 1, c_s, c_r).wait_send()
    scores_in().wait_send()
    many(half, half_rows, s0, s0).wait_send()
    many(part, n_pa - 1, s1, r1).wait_send()
    if n_z > 1:
        many(got2, n_z - 1, s2, r2).wait_send()
    many(out, chunk * (n_pa - 1), s4, s4).wait_send()
    many(out, half_rows, s5, r5).wait_send()


def hand_over(loss_ref, qg_ref, pg_ref, wg_ref, loss_out, qg_out, pg_out, wg_out):
    loss_out[...] = loss_ref[:, 0:loss_out.shape[1]]
    qg_out[...] = qg_ref[...]
    pg_out[...] = pg_ref[...]
    wg_out[...] = wg_ref[...].astype(F32)


def shards(query_hidden, passage_hidden, projection, candidates):
    queries, qlen, width = query_hidden.shape
    n_p, plen, _ = passage_hidden.shape
    vec = projection.shape[1]
    n_pa, n_z = lax.axis_size("pa"), lax.axis_size("pb") // 2
    rows_q, rows_p = queries * qlen, n_p * plen
    all_rows = n_pa * rows_q
    hrow = rows_q // 2
    half_rows = width // 2
    chunk = half_rows // n_pa
    dma = pltpu.SemaphoreType.DMA
    V = pltpu.VMEM
    in_vmem, anywhere = pl.BlockSpec(memory_space=pltpu.VMEM), pl.BlockSpec(memory_space=pl.ANY)
    loss, query_grad, passage_grad, weight_grad = pl.pallas_call(
        functools.partial(kernel, n_z, qlen, candidates.shape[1]),
        out_shape=(
            jax.ShapeDtypeStruct((1, 128), F32),
            jax.ShapeDtypeStruct((rows_q, vec), F32),
            jax.ShapeDtypeStruct((rows_p, vec), F32),
            jax.ShapeDtypeStruct((width, vec), BF16),
        ),
        in_specs=[anywhere, anywhere, anywhere, in_vmem],
        out_specs=(in_vmem,) * 4,
        scratch_shapes=[
            V((width, vec), BF16), V((rows_q, width), BF16), V((rows_p, width), BF16), V((rows_q, vec), F32), V((rows_p, vec), F32),
            V((n_p, vec, plen), BF16), V((n_p, plen, 2 * vec), BF16), V((n_pa, rows_q, vec), BF16),
            V((n_p, all_rows, plen), BF16), V((n_p, all_rows, vec), BF16), V((n_p, all_rows, vec), BF16),
            V((n_p, 2, 8, 128), F32), V((n_pa, 16, 128), BF16), V((n_pa, 8, 256), F32), V((n_pa, 8, 256), F32),
            V((n_pa, 8, 256), F32), V((n_p, 256, vec), F32),
            V((10, hrow, vec), BF16), V((20, hrow, vec), BF16), V((10, hrow, vec), BF16), V((20, hrow, vec), BF16),
            V((2 * SIDE, hrow, vec), F32), V((n_p, vec, plen), F32), V((vec, rows_q), BF16), V((vec, rows_p), BF16),
            V((width, vec), F32), V((width, vec), BF16), V((half_rows, vec), BF16), V((half_rows, vec), BF16),
            V((n_pa, chunk, vec), BF16), V((n_pa, chunk, vec), BF16), V((chunk, vec), F32), V((n_z, chunk, vec), BF16),
            dma((3 + n_p,)), dma, dma, dma, dma, dma, dma((40,)), dma, dma((40,)),
            dma, dma((SIDE,)), dma, dma, dma, dma, dma, dma((n_pa,)), dma, dma,
        ],
        compiler_params=pltpu.CompilerParams(collective_id=0, has_side_effects=True, vmem_limit_bytes=60 * 2**20),
        name="retriever",
    )(query_hidden.reshape(rows_q, width), passage_hidden.reshape(rows_p, width), projection, candidates)
    loss, query_grad, passage_grad, weight_grad = pl.pallas_call(
        hand_over,
        out_shape=(
            jax.ShapeDtypeStruct((1, queries), F32),
            jax.ShapeDtypeStruct((rows_q, vec), F32),
            jax.ShapeDtypeStruct((rows_p, vec), F32),
            jax.ShapeDtypeStruct((width, vec), F32),
        ),
        in_specs=[in_vmem] * 4,
        out_specs=(in_vmem,) * 4,
        name="hand_over",
    )(loss, query_grad, passage_grad, weight_grad)
    return (
        loss.reshape(queries),
        query_grad.reshape(queries, qlen, vec),
        passage_grad.reshape(n_p, plen, vec),
        weight_grad,
    )


def solution(mesh):
    placed = (P(("pb", "pa"), None, None), P(("pb", "pa"), None, None), P(), P(("pb", "pa"), None))
    return jax.shard_map(
        shards,
        mesh=mesh,
        in_specs=placed,
        out_specs=(P(("pb", "pa")), P(("pb", "pa"), None, None), P(("pb", "pa"), None, None), P()),
        check_vma=False,
    )
```

```python
import functools
import jax
import jax.numpy as jnp
from jax import lax
from jax.experimental import pallas as pl
from jax.experimental.pallas import tpu as pltpu
from jax.sharding import PartitionSpec as P

MESH = pl.DeviceIdType.MESH
F32, BF16 = jnp.float32, jnp.bfloat16
SIDE = 4
sharpness_divisor = 0.1
epsilon = 1e-06
LOG2E = 1.4426950408889634


def remote(src, dst, send, recv, device):
    return pltpu.make_async_remote_copy(
        src_ref=src, dst_ref=dst, send_sem=send, recv_sem=recv, device_id=device, device_id_type=MESH
    )


def dot(a, b, ca=1, cb=0):
    return lax.dot_general(a, b, (((ca,), (cb,)), ((), ())), preferred_element_type=F32)


def inverse_norm(embedded):
    return lax.rsqrt(jnp.mean(embedded * embedded, axis=-1, keepdims=True) + epsilon)


def norm_backward(embedded, unit_grad):
    inv_norm = inverse_norm(embedded)
    inner_mean = jnp.mean(embedded * unit_grad, axis=-1, keepdims=True)
    return inv_norm * unit_grad - inv_norm * inv_norm * inv_norm * embedded * inner_mean


def pick(k, values):
    result = values[0]
    for i, v in enumerate(values[1:]):
        result = jnp.where(k == i + 1, v, result)
    return result


FAR = [10, 9, 11, 6, 14, 2, 8, 5, 7, 13, 15, 1, 3, 4, 12]
ORDER = [(0, 0), (1, 0), (3, 0), (0, 1), (0, 3), (1, 1), (1, 3), (3, 1), (3, 3),
         (2, 0), (0, 2), (2, 1), (2, 3), (1, 2), (3, 2), (2, 2)]


def kernel(n_z, qlen, cand_count,
           qh_ref, ph_ref, proj_ref, cand_ref,
           loss_ref, qg_ref, pg_ref, wg_ref,
           proj, qh, ph, qe, pe, pt, pone, gq, ex, gn, qn, acc, cbuf, mask, mark, score, gsrep,
           sbuf1, sbuf2, rbuf1, rbuf2, sum1, gp, qgb, pgb,
           wg, out, half, got0, part, got1, mine, got2,
           sem_h, c_s, c_r, sc_s, sc_r, a_s, a_r, b_s, b_r,
           s0, r0, s1, r1, s2, r2, s4, r4, s5, r5):
    n_pa = SIDE * SIDE
    rows_q = qh.shape[0]
    hrow = rows_q // 2
    qrow = hrow // 2
    queries = rows_q // qlen
    n_p, plen = pone.shape[0], pone.shape[1]
    width = qh.shape[1]
    vec = proj.shape[1]
    me, pb = lax.axis_index("pa"), lax.axis_index("pb")
    y, x = me // SIDE, me % SIDE
    z, core = pb // 2, pb % 2
    partner = {"pb": z * 2 + (1 - core)}
    scale = 1.0 / (vec * sharpness_divisor)

    rows = [lax.rem(y + d, SIDE) * SIDE for d in range(SIDE)]
    columns = [lax.rem(x + d, SIDE) for d in range(SIDE)]
    at_offset = [rows[k // SIDE] + columns[k % SIDE] for k in range(n_pa)]
    along_z = [lax.rem(z + k, n_z) for k in range(n_z)]

    def back(k):
        return (SIDE - k // SIDE) % SIDE * SIDE + (SIDE - k % SIDE) % SIDE

    def plane(k):
        return {"pa": at_offset[k]}

    def line_z(k):
        return {"pb": along_z[k] * 2 + core}

    def load_q(k):
        at = pl.ds(k * hrow, hrow)
        return pltpu.make_async_copy(qh_ref.at[at], qh.at[at], sem_h.at[k])

    def load_p(k):
        at = pl.ds(k * plen, plen)
        return pltpu.make_async_copy(ph_ref.at[at], ph.at[at], sem_h.at[2 + k])

    load_w = pltpu.make_async_copy(proj_ref, proj, sem_h.at[2 + n_p])
    load_w.start()
    for k in range(2):
        load_q(k).start()

    barrier = pltpu.get_barrier_semaphore()
    pl.semaphore_signal(barrier, inc=1, device_id=partner, device_id_type=MESH)

    for k in range(1, n_pa):
        pl.semaphore_signal(barrier, inc=1, device_id=plane(k), device_id_type=MESH)
    for k in range(1, n_z):
        pl.semaphore_signal(barrier, inc=1, device_id=line_z(k), device_id_type=MESH)

    for k in range(n_p):
        load_p(k).start()

    lane = lax.broadcasted_iota(jnp.int32, (queries, 128), 1)
    line = lax.broadcasted_iota(jnp.int32, (queries, 128), 0)
    place = (lane == line + (me % 8) * queries).astype(F32)
    cbuf[me] = jnp.concatenate([dot(cand_ref[...].astype(F32), place, 0, 0), jnp.zeros((16 - cand_count, 128), F32)], axis=0).astype(BF16)
    score[...] = jnp.zeros_like(score)
    acc[...] = jnp.zeros_like(acc)

    def shift(h, d1, d2):
        dx, dy = (d1, d2) if h == 0 else (d2, d1)
        return dy % SIDE * SIDE + dx % SIDE

    def slot(h, d1, d2):
        return at_offset[shift(h, d1, d2)]

    def neighbour(h, g, o):
        return plane(shift(h, o, 0) if g == 0 else shift(h, 0, o))

    def piece_of(h, g, o, k, to, first, count):
        d1, d2 = (o, 0) if g == 0 else (g - 1, o)
        block = gq.at[slot(h, d1, d2), pl.ds(h * hrow + first, count)]
        return remote(block, block, a_s, a_r.at[(h * 5 + g) * 4 + k], neighbour(h, g, to))

    def whole(h, g, o, k, to):
        return piece_of(h, g, o, k, to, 0, hrow)

    def quarter(h, g, o, k, to):
        return piece_of(h, g, o, k, to, (k - 2) * qrow, qrow)

    def send_whole(h, g):
        whole(h, g, 0, 0, 1).start()
        whole(h, g, 0, 1, 3).start()

    def pass_on(h, g):
        whole(h, g, 3, 0, 1).wait_recv()
        quarter(h, g, 3, 2, 1).start()
        whole(h, g, 1, 1, 3).wait_recv()
        quarter(h, g, 1, 3, 3).start()

    def finish(h, g):
        quarter(h, g, 2, 2, 1).wait_recv()
        quarter(h, g, 2, 3, 3).wait_recv()

    def to_all(buf, send, recv):
        for k in FAR:
            remote(buf, buf, send, recv, plane(k)).start()

    def scores_in():
        part_of = score.at[pl.ds(0, n_pa - 1), pl.ds(0, 4)]
        return remote(part_of, part_of, sc_s, sc_r, partner)

    def many(buf, count, send, recv):
        part_of = buf.at[pl.ds(0, count)]
        return remote(part_of, part_of, send, recv, partner)

    for h in range(2):
        at = pl.ds(h * hrow, hrow)
        if h == 0:
            load_w.wait()
        load_q(h).wait()
        e = dot(qh[at, :], proj[...])
        qe[at, :] = e
        gq[me, at, :] = (e * inverse_norm(e)).astype(BF16)
        if h == 0:
            pl.semaphore_wait(barrier, n_pa + n_z - 1)
        send_whole(h, 0)
        send_whole(h, 1)

    to_all(cbuf.at[me], c_s, c_r)

    def project_passage(k):
        load_p(k).wait()
        at = pl.ds(k * plen, plen)
        e = dot(ph[at, :], proj[...])
        pe[at, :] = e
        u = (e * inverse_norm(e)).astype(BF16)
        pone[k, :, 0:vec] = u
        pone[k, :, vec:] = jnp.ones((plen, vec), BF16)
        pt[k] = u.astype(F32).T.astype(BF16)

    project_passage(0)

    project_passage(1)

    for h in range(2):
        pass_on(h, 0)
        send_whole(h, 2)
        send_whole(h, 4)

    for k in range(2, n_p):
        project_passage(k)

    narrow = lax.broadcasted_iota(jnp.int32, (8, 128), 1)

    @pl.loop(0, n_pa)
    def _(k):
        @pl.when(k == 1)
        def _():
            for h in range(2):
                pass_on(h, 1)

        @pl.when(k == 3)
        def _():
            for h in range(2):
                finish(h, 0)
                send_whole(h, 3)

        @pl.when(k == 5)
        def _():
            for h in range(2):
                pass_on(h, 2)
                pass_on(h, 4)

        @pl.when(k == 9)
        def _():
            for h in range(2):
                pass_on(h, 3)

        @pl.when(k == 9)
        def _():
            for h in range(2):
                finish(h, 1)

        @pl.when(k == 11)
        def _():
            for h in range(2):
                finish(h, 2)
                finish(h, 4)

        @pl.when(k == 15)
        def _():
            for h in range(2):
                finish(h, 3)

        b = pick(k, [at_offset[dy * SIDE + dx] for dx, dy in ORDER])
        u = gq[b]
        at = pl.ds(pl.multiple_of(b * rows_q, rows_q), rows_q)
        for p in range(n_p):
            e = jnp.exp2(dot(u, pt[p]) * (LOG2E * scale)).astype(BF16)
            ex[p, at, :] = e
            sums = dot(e, pone[p])
            total = sums[:, vec:]
            inverse = 1.0 / total
            gn[p, at, :] = (sums[:, :vec] * inverse).astype(BF16)
            qn[p, at, :] = (u.astype(F32) * inverse).astype(BF16)
            four = total.reshape(queries, 4, qlen // 4, vec)
            logs = jnp.log((four[:, 0] * four[:, 1]) * (four[:, 2] * four[:, 3]))
            s = acc[p, b // 8]
            for i in range(queries):
                s = s + jnp.where(narrow == lax.rem(b, 8) * queries + i, logs[i], 0.0)
            acc[p, b // 8] = s

    for p in range(n_p):
        for i in range(2):
            score[me, p:p + 1, i * 128:(i + 1) * 128] = sharpness_divisor * jnp.sum(acc[p, i], axis=0, keepdims=True)

    to_all(score.at[me, pl.ds(0, 4)], sc_s, sc_r)
    many(cbuf, n_pa - 1, c_s, c_r).wait_recv()

    left, right = cbuf[0].astype(F32), cbuf[8].astype(F32)
    for i in range(1, 8):
        left = left + cbuf[i].astype(F32)
        right = right + cbuf[8 + i].astype(F32)
    named = jnp.concatenate([left, right], axis=1).astype(jnp.int32)
    rank = lax.broadcasted_iota(jnp.int32, (8, 256), 0)

    @pl.loop(0, n_pa)
    def _(o):
        ident = jnp.where(rank < n_p, o * n_p + rank, -1)
        first = (named[0:1, :] == ident).astype(F32)
        found = first
        for c in range(1, cand_count):
            found = found + (named[c:c + 1, :] == ident).astype(F32)
        mask[o] = found
        mark[o] = first

    scores_in().wait_recv()

    similarity = score[...]
    exponent = jnp.exp(similarity) * mask[...]
    element_total = jnp.sum(jnp.sum(exponent, axis=0), axis=0, keepdims=True)
    chosen = jnp.sum(jnp.sum(similarity * mark[...], axis=0), axis=0, keepdims=True)
    loss = jnp.log(element_total) - chosen
    mine_row = lax.broadcasted_iota(jnp.int32, (queries, 256), 1) == lax.broadcasted_iota(
        jnp.int32, (queries, 256), 0) + me * queries
    column = jnp.sum(jnp.where(mine_row, loss, 0.0), axis=1, keepdims=True)
    loss_ref[...] = jnp.sum(jnp.where(lane == line, column, 0.0), axis=0, keepdims=True)
    grad_score = (jnp.exp(score[me]) * mask[me] / element_total - mark[me]) * (1.0 / vec)
    for p in range(n_p):
        gsrep[p] = jnp.broadcast_to(grad_score[p:p + 1, :], (vec, 256)).T

    q_half = queries // 2

    def spread(p, b, h, count):
        g = gsrep[p, pl.ds(pl.multiple_of(b * queries + h * q_half, 8), count), :]
        return jnp.broadcast_to(g[:, None, :], (count, qlen, vec)).reshape(count * qlen, vec)

    def value(h, g, o):
        if g == 0:
            return sum1[h * SIDE + o]
        b = slot(h, g - 1, o)
        at = pl.ds(pl.multiple_of(b * rows_q + h * hrow, hrow), hrow)
        result = spread(0, b, h, q_half) * gn[0, at, :].astype(F32)
        for p in range(1, n_p):
            result = result + spread(p, b, h, q_half) * gn[p, at, :].astype(F32)
        return result

    def leg1(h, g, k, to):
        i = h * 5 + g
        at = pl.ds(k * qrow, qrow)
        return remote(sbuf1.at[i, at], rbuf1.at[i, at], b_s, b_r.at[i * 4 + k], neighbour(h, g, to))

    def leg2(h, g, k, to):
        i = h * 5 + g
        return remote(sbuf2.at[i * 2 + k], rbuf2.at[i * 2 + k], b_s, b_r.at[i * 4 + 2 + k],
                      neighbour(h, g, to))

    def step1(h, g):
        sbuf1[h * 5 + g] = value(h, g, 2).astype(BF16)
        leg1(h, g, 0, 1).start()
        leg1(h, g, 1, 3).start()

    def step2(h, g):
        i = h * 5 + g
        v = value(h, g, 1)
        leg1(h, g, 0, 1).wait_recv()
        sbuf2[i * 2, 0:qrow, :] = (v[0:qrow] + rbuf1[i, 0:qrow, :].astype(F32)).astype(BF16)
        sbuf2[i * 2, qrow:, :] = v[qrow:].astype(BF16)
        leg2(h, g, 0, 1).start()
        v = value(h, g, 3)
        leg1(h, g, 1, 3).wait_recv()
        sbuf2[i * 2 + 1, 0:qrow, :] = v[0:qrow].astype(BF16)
        sbuf2[i * 2 + 1, qrow:, :] = (v[qrow:] + rbuf1[i, qrow:, :].astype(F32)).astype(BF16)
        leg2(h, g, 1, 3).start()

    def step3(h, g):
        i = h * 5 + g
        v = value(h, g, 0)
        leg2(h, g, 0, 1).wait_recv()
        v = v + rbuf2[i * 2].astype(F32)
        leg2(h, g, 1, 3).wait_recv()
        return v + rbuf2[i * 2 + 1].astype(F32)

    def grad_passage(first, last):
        @pl.loop(first, last)
        def _(b):
            at = pl.ds(pl.multiple_of(b * rows_q, rows_q), rows_q)
            for p in range(n_p):
                w = (spread(p, b, 0, queries) * qn[p, at, :].astype(F32)).astype(BF16)
                gp[p] += dot(w.T, ex[p, at, :])

    gp[...] = jnp.zeros_like(gp)

    for i in range(8):
        step1(i % 2, 1 + (i // 2 + 2) % SIDE)

    grad_passage(0, 5)

    for i in range(8):
        step2(i % 2, 1 + (i // 2 + 2) % SIDE)

    grad_passage(5, 16)

    for h in range(2):
        sum1[h * SIDE + 2] = step3(h, 3)
        step1(h, 0)

    for p in range(n_p):
        at = pl.ds(p * plen, plen)
        g = norm_backward(pe[at, :], gp[p].T)
        pg_ref[at, :] = g
        pgb[:, at] = g.T.astype(BF16)

    quarter_rows = width // 8

    def passage_product(first, last):
        @pl.loop(first, last)
        def _(c):
            at = pl.ds(pl.multiple_of(c * quarter_rows, quarter_rows), quarter_rows)
            wg[at, :] = dot(pgb[...], ph[:, at]).T

    passage_product(0, 3)

    for h in range(2):
        sum1[h * SIDE + 1] = step3(h, 2)
        sum1[h * SIDE + 3] = step3(h, 4)
        step2(h, 0)
        sum1[h * SIDE] = step3(h, 1)

    passage_product(3, 8)

    for h in range(2):
        at = pl.ds(h * hrow, hrow)
        g = norm_backward(qe[at, :], step3(h, 0))
        qg_ref[at, :] = g
        qgb[:, at] = g.T.astype(BF16)

    half_rows = width // 2
    chunk = half_rows // n_pa
    base = core * half_rows

    def swap(j):
        at = pl.ds(pl.multiple_of(lax.rem(y + 1 + j, SIDE) * quarter_rows, quarter_rows), quarter_rows)
        return remote(half.at[at], got0.at[at], s0, r0.at[j], partner)

    def product(first, j):
        at = pl.ds(pl.multiple_of(first + lax.rem(y + 1 + j, SIDE) * quarter_rows, quarter_rows), quarter_rows)
        return wg[at, :] + dot(qgb[...], qh[:, at]).T

    @pl.loop(0, SIDE)
    def _(j):
        at = pl.ds(pl.multiple_of(lax.rem(y + 1 + j, SIDE) * quarter_rows, quarter_rows), quarter_rows)
        half[at, :] = product(half_rows - base, j).astype(BF16)
        swap(j).start()

    def to_xy(peer):
        return remote(part.at[peer], got1.at[me], s1, r1, {"pa": peer})

    @pl.loop(0, SIDE)
    def _(j):
        v = product(base, j)
        row = lax.rem(y + 1 + j, SIDE)
        swap(j).wait_recv()
        v = v + got0[pl.ds(pl.multiple_of(row * quarter_rows, quarter_rows), quarter_rows), :].astype(F32)
        for i in range(SIDE):
            part[row * SIDE + i] = v[i * chunk:(i + 1) * chunk].astype(BF16)

            @pl.when((row == y) & (x == i))
            def _():
                mine[...] = v[i * chunk:(i + 1) * chunk]

        for i in range(1, SIDE):
            to_xy(row * SIDE + columns[i]).start()

        @pl.when(j < SIDE - 1)
        def _():
            to_xy(row * SIDE + x).start()

    many(got1, n_pa - 1, s1, r1).wait_recv()
    total = mine[...]
    for k in range(1, n_pa):
        total = total + got1[at_offset[k]].astype(F32)
    total = total.astype(BF16)
    part[me] = total
    got2[z] = total
    for k in range(1, n_z):
        remote(part.at[me], got2.at[z], s2, r2, line_z(k)).start()
    if n_z > 1:
        many(got2, n_z - 1, s2, r2).wait_recv()
    total = got2[0].astype(F32)
    for k in range(1, n_z):
        total = total + got2[k].astype(F32)
    out[pl.ds(base + me * chunk, chunk), :] = total.astype(BF16)

    def chunk_at(first, who):
        return out.at[pl.ds(first + who * chunk, chunk)]

    def back_xy(k, who, recv):
        return remote(chunk_at(base, who), chunk_at(base, who), s4, r4.at[recv], plane(k))

    def across(k):
        here = chunk_at(base, at_offset[k])
        return remote(here, here, s5, r5, partner)

    for k in FAR:
        back_xy(k, me, back(k)).start()
    across(0).start()
    for k in FAR[::-1]:
        back_xy(k, at_offset[k], k).wait_recv()
        across(k).start()
    many(out, half_rows, s5, r5).wait_recv()
    wg_ref[...] = out[...]

    many(gq, n_pa - 1, a_s, a_s).wait_send()
    many(sbuf1, 10, b_s, b_s).wait_send()
    many(sbuf2, 20, b_s, b_s).wait_send()
    many(cbuf, n_pa - 1, c_s, c_r).wait_send()
    scores_in().wait_send()
    many(half, half_rows, s0, s0).wait_send()
    many(part, n_pa - 1, s1, r1).wait_send()
    if n_z > 1:
        many(got2, n_z - 1, s2, r2).wait_send()
    many(out, chunk * (n_pa - 1), s4, s4).wait_send()
    many(out, half_rows, s5, r5).wait_send()


def hand_over(loss_ref, qg_ref, pg_ref, wg_ref, loss_out, qg_out, pg_out, wg_out):
    loss_out[...] = loss_ref[:, 0:loss_out.shape[1]]
    qg_out[...] = qg_ref[...]
    pg_out[...] = pg_ref[...]
    wg_out[...] = wg_ref[...].astype(F32)


def shards(query_hidden, passage_hidden, projection, candidates):
    queries, qlen, width = query_hidden.shape
    n_p, plen, _ = passage_hidden.shape
    vec = projection.shape[1]
    n_pa, n_z = lax.axis_size("pa"), lax.axis_size("pb") // 2
    rows_q, rows_p = queries * qlen, n_p * plen
    all_rows = n_pa * rows_q
    hrow = rows_q // 2
    half_rows = width // 2
    chunk = half_rows // n_pa
    dma = pltpu.SemaphoreType.DMA
    V = pltpu.VMEM
    in_vmem, anywhere = pl.BlockSpec(memory_space=pltpu.VMEM), pl.BlockSpec(memory_space=pl.ANY)
    loss, query_grad, passage_grad, weight_grad = pl.pallas_call(
        functools.partial(kernel, n_z, qlen, candidates.shape[1]),
        out_shape=(
            jax.ShapeDtypeStruct((1, 128), F32),
            jax.ShapeDtypeStruct((rows_q, vec), F32),
            jax.ShapeDtypeStruct((rows_p, vec), F32),
            jax.ShapeDtypeStruct((width, vec), BF16),
        ),
        in_specs=[anywhere, anywhere, anywhere, in_vmem],
        out_specs=(in_vmem,) * 4,
        scratch_shapes=[
            V((width, vec), BF16), V((rows_q, width), BF16), V((rows_p, width), BF16), V((rows_q, vec), F32), V((rows_p, vec), F32),
            V((n_p, vec, plen), BF16), V((n_p, plen, 2 * vec), BF16), V((n_pa, rows_q, vec), BF16),
            V((n_p, all_rows, plen), BF16), V((n_p, all_rows, vec), BF16), V((n_p, all_rows, vec), BF16),
            V((n_p, 2, 8, 128), F32), V((n_pa, 16, 128), BF16), V((n_pa, 8, 256), F32), V((n_pa, 8, 256), F32),
            V((n_pa, 8, 256), F32), V((n_p, 256, vec), F32),
            V((10, hrow, vec), BF16), V((20, hrow, vec), BF16), V((10, hrow, vec), BF16), V((20, hrow, vec), BF16),
            V((2 * SIDE, hrow, vec), F32), V((n_p, vec, plen), F32), V((vec, rows_q), BF16), V((vec, rows_p), BF16),
            V((width, vec), F32), V((width, vec), BF16), V((half_rows, vec), BF16), V((half_rows, vec), BF16),
            V((n_pa, chunk, vec), BF16), V((n_pa, chunk, vec), BF16), V((chunk, vec), F32), V((n_z, chunk, vec), BF16),
            dma((3 + n_p,)), dma, dma, dma, dma, dma, dma((40,)), dma, dma((40,)),
            dma, dma((SIDE,)), dma, dma, dma, dma, dma, dma((n_pa,)), dma, dma,
        ],
        compiler_params=pltpu.CompilerParams(collective_id=0, has_side_effects=True, vmem_limit_bytes=60 * 2**20),
        name="retriever",
    )(query_hidden.reshape(rows_q, width), passage_hidden.reshape(rows_p, width), projection, candidates)
    loss, query_grad, passage_grad, weight_grad = pl.pallas_call(
        hand_over,
        out_shape=(
            jax.ShapeDtypeStruct((1, queries), F32),
            jax.ShapeDtypeStruct((rows_q, vec), F32),
            jax.ShapeDtypeStruct((rows_p, vec), F32),
            jax.ShapeDtypeStruct((width, vec), F32),
        ),
        in_specs=[in_vmem] * 4,
        out_specs=(in_vmem,) * 4,
        name="hand_over",
    )(loss, query_grad, passage_grad, weight_grad)
    return (
        loss.reshape(queries),
        query_grad.reshape(queries, qlen, vec),
        passage_grad.reshape(n_p, plen, vec),
        weight_grad,
    )


def solution(mesh):
    placed = (P(("pb", "pa"), None, None), P(("pb", "pa"), None, None), P(), P(("pb", "pa"), None))
    return jax.shard_map(
        shards,
        mesh=mesh,
        in_specs=placed,
        out_specs=(P(("pb", "pa")), P(("pb", "pa"), None, None), P(("pb", "pa"), None, None), P()),
        check_vma=False,
    )
```
